256 devices in a mesh: dp: 8 (over z), expert: 32 (over y, x, core).
Axes of the slice: x: 4, y: 4, z: 8, core: 2. Of those that a mesh axis runs over, the one named last changes fastest.
Arguments:
- inputs: bfloat16 [32768, 2048], P(('dp', 'expert')), may hold values from -6 to 6
- out_grad: bfloat16 [32768, 2048], P(('dp', 'expert')), may hold values from -6 to 6
- route_weights: bfloat16 [32768, 8], P(('dp', 'expert')), may hold values from 0.019897461 to 0.5
- routes: int32 [32768, 8], P(('dp', 'expert')), may hold values from 0 to 63, all different within a row; in each aligned block of 128 rows (0 to 127, 128 to 255, ...) at most 18 rows name the same one
- response_counts: int32 [256], P(('dp', 'expert')), may hold values from 1 to 128, 16384 in all
- gate_weight: bfloat16 [64, 2048, 384], P('expert'), may hold values from -0.125 to 0.125
- up_weight: bfloat16 [64, 2048, 384], P('expert'), may hold values from -0.125 to 0.125
- down_weight: bfloat16 [64, 384, 2048], P('expert'), may hold values from -0.3125 to 0.3125
Outputs:
- in_grad: bfloat16 [32768, 2048], P(('dp', 'expert'))
- gate_grad: bfloat16 [64, 2048, 384], P('expert', 'dp')
- up_grad: bfloat16 [64, 2048, 384], P('expert', 'dp')
- down_grad: bfloat16 [64, 384, 2048], P('expert', None, 'dp')
- route_weight_grad: bfloat16 [32768, 8], P(('dp', 'expert'))
The draws below stay inside these ranges and needn't reach their ends.
Inputs may be any that keep to these rules, and one draw needn't show every extreme that they name: `routes`: among the 128 tokens of one device, no expert is named by more than 18 slots, a bound that some block reaches. A token names 8 different experts.
All inputs are finite; a program needn't handle non-finite values. No bound on the sum of `response_counts` on one device may be relied on, other than what follows from the above.
Results may differ from the reference program's by a relative error of at most 0.019.
Values may be sent and summed in bfloat16 or wider, within the bound.
A program may use at most 128 MiB of HBM per device.

```python
import math
import jax
import jax.numpy as jnp
import numpy as np
from jax import lax

D = 2048
FF = 384
TOP = 8
TOK_DEV = 128
EXPERTS = 64
MOST = 18
TOKENS = 32768
N_DP = 8
N_EXPERT = 32


def block_levels(stream_key, shape, shards, smallest, top_value):
    loudness = 1.0
    for axis_at, shards_of in shards:
        draws = jax.random.uniform(jax.random.fold_in(jax.random.fold_in(stream_key, 6), axis_at), (shards_of,), jnp.float32, smallest / len(shards), top_value / len(shards))
        loudness = loudness * jnp.repeat(jnp.exp(draws), shape[axis_at] // shards_of).reshape((-1,) + (1,) * (len(shape) - 1 - axis_at))
    return loudness


def profile(amount, total, limit, lean):
    portions = [(1 << 20) // math.isqrt(grade ** lean) + 1 for grade in range(2, amount + 1)]
    surplus, holding = total - limit - (amount - 1), [1] * (amount - 1)
    while surplus > 0:
        free = [i for i in range(amount - 1) if holding[i] < limit]
        pool, left = sum([portions[i] for i in free]), surplus
        for i in free:
            extra = min(limit - holding[i], max(1, left * portions[i] // pool), surplus)
            holding[i] = holding[i] + extra
            surplus = surplus - extra
    return np.array([limit] + holding)


def uneven(stream_key, amount, total, reach, skew):
    if amount == 2:
        one = jax.random.randint(stream_key, (), max(1, total - reach), min(reach, total - 1) + 1)
        return jnp.stack([one, total - one])
    lengths = jnp.asarray(profile(amount, total, reach, skew), jnp.int32)
    twos = (amount - 1) // 2
    source_of, receiver = lengths[1:1 + 2 * twos:2], lengths[2:2 + 2 * twos:2]
    margin = jnp.minimum(source_of - 1, reach - receiver)
    moved = jax.random.randint(jax.random.fold_in(stream_key, 1), (twos,), 0, 1 << 20) % (margin + 1)
    lengths = lengths.at[1:1 + 2 * twos:2].set(source_of - moved).at[2:2 + 2 * twos:2].set(receiver + moved)
    return lengths[jax.random.permutation(jax.random.fold_in(stream_key, 2), amount)]


def shared_out(key, own, number, rows, number_of, top, reach, skew):
    ranking = jax.random.permutation(key, number_of)
    packed, ordinary = load_shares(number_of, rows * top, reach, skew, True), load_shares(number_of, rows * top, reach, skew, False)
    places = jnp.arange(number_of)

    def named(sizes, turn):
        used = int((sizes > 0).sum())
        fixed = max(1, used // 4)
        passed = fixed + (places - fixed + turn * (used - fixed)) % max(1, number_of - fixed)
        return jnp.zeros((number_of,), jnp.int32).at[ranking[jnp.where(places < fixed, places, passed)]].set(jnp.asarray(sizes, jnp.int32))

    sizes = jnp.where(number % 4 == 0, named(packed, number // 4), named(ordinary, number - number // 4 - 1))
    mixed = jax.random.permutation(jax.random.fold_in(own, 3), number_of)
    donor, taker = mixed[0:number_of // 2 * 2:2], mixed[1:number_of // 2 * 2:2]
    margin = jnp.minimum(sizes[donor] - 1, reach - sizes[taker]) // 2
    margin = jnp.where((donor == ranking[0]) | (taker == ranking[0]) | (sizes[taker] == 0), 0, jnp.maximum(margin, 0))
    passed = jax.random.randint(jax.random.fold_in(own, 4), (number_of // 2,), 0, 1 << 20) % (margin + 1)
    sizes = sizes.at[donor].add(-passed).at[taker].add(passed)
    items = jnp.searchsorted(jnp.cumsum(sizes), jnp.arange(rows * top), side="right").astype(jnp.int32)
    listing = items.reshape(top, rows).T
    listing = listing[jax.random.permutation(jax.random.fold_in(own, 1), rows)]
    turn = jax.random.randint(jax.random.fold_in(own, 2), (rows, 1), 0, top)
    return jnp.take_along_axis(listing, (jnp.arange(top)[None, :] + turn) % top, axis=1)


def load_shares(count, total, limit, lean, full):
    loads = [(1 << 20) // math.isqrt(rank ** lean) + 1 for rank in range(1, count + 1)]
    largest = limit if full else min(limit, max(-(-total // count), total * loads[0] // sum(loads)))
    least = 1 if total - largest >= count - 1 else 0
    given, surplus = [largest] + [least] * (count - 1), total - largest - least * (count - 1)
    while surplus > 0:
        free = [i for i in range(1, count) if given[i] < largest] or [i for i in range(1, count) if given[i] < limit]
        mass, left = sum([loads[i] for i in free]), surplus
        for i in free:
            more = min(limit - given[i], max(1, left * loads[i] // mass), surplus)
            given[i] = given[i] + more
            surplus = surplus - more
    return np.array(given)


def scatter_about(stream_key, extent, spread, most, shards=(), kind=jnp.bfloat16):
    factor_of = block_levels(stream_key, extent, shards, -0.22, 0.18) if shards else 1.0
    drawn = jax.random.normal(stream_key, extent, jnp.float32) * spread * factor_of
    return jnp.minimum(jnp.maximum(drawn, -most), most).astype(kind)


def setup_inputs(seed: int = 0) -> dict:
    key_list = jax.random.split(jax.random.key(seed), 9)
    inputs = scatter_about(key_list[0], (TOKENS, D), 1.0, 6.0, ((0, 256),))
    out_grad = scatter_about(key_list[1], (TOKENS, D), 1.0, 6.0, ((0, 256),))
    route_weights = jnp.clip(jnp.exp(math.log(0.5) - 3.224016 * jax.random.uniform(key_list[2], (TOKENS, TOP), jnp.float32) ** block_levels(key_list[2], (TOKENS, TOP), ((0, 256),), -0.2, 0.2)), 0.019897461, 0.5).astype(jnp.bfloat16)
    routes_keys = jax.random.split(jax.random.fold_in(key_list[3], 1), TOKENS // TOK_DEV)
    routes_turns = jax.random.permutation(jax.random.fold_in(key_list[3], 3), TOKENS // TOK_DEV)
    routes = jax.vmap(lambda own, number: shared_out(jax.random.fold_in(key_list[3], 2), own, number, TOK_DEV, EXPERTS, TOP, MOST, 2))(routes_keys, routes_turns).reshape((TOKENS, TOP))
    response_counts = uneven(key_list[4], N_DP * N_EXPERT, N_DP * N_EXPERT * TOK_DEV // 2, TOK_DEV, 2).astype(jnp.int32)
    gate_weight = scatter_about(key_list[5], (EXPERTS, D, FF), D ** -0.5, 0.125, ((0, 32),))
    up_weight = scatter_about(key_list[6], (EXPERTS, D, FF), D ** -0.5, 0.125, ((0, 32),))
    down_weight = scatter_about(key_list[7], (EXPERTS, FF, D), FF ** -0.5, 0.3125, ((0, 32),))
    return dict(inputs=inputs, out_grad=out_grad, route_weights=route_weights, routes=routes, response_counts=response_counts, gate_weight=gate_weight, up_weight=up_weight, down_weight=down_weight)


def silu_parts(gate_pre):
    sigmoid_val = jax.nn.sigmoid(gate_pre)
    return gate_pre * sigmoid_val, sigmoid_val * (1.0 + gate_pre * (1.0 - sigmoid_val))


def reference(inputs, out_grad, route_weights, routes, response_counts, gate_weight, up_weight, down_weight):
    tokens_all, model_width = inputs.shape
    blocks = tokens_all // TOK_DEV
    slot_count = TOK_DEV * TOP
    positions = jnp.arange(tokens_all, dtype=jnp.int32)
    block_of = positions // TOK_DEV
    live_rows = (positions % TOK_DEV >= TOK_DEV - response_counts[block_of]).astype(out_grad.dtype)
    masked = out_grad * live_rows[:, None]
    block_routes = routes.reshape(blocks, slot_count)
    onehot = (block_routes[:, :, None] == jnp.arange(EXPERTS, dtype=jnp.int32)[None, None, :]).astype(jnp.int32)
    slot_rank = jnp.sum(onehot * jnp.cumsum(onehot, axis=1), axis=2) - 1
    target = block_routes * MOST + slot_rank
    block_ids = jnp.broadcast_to(jnp.arange(blocks, dtype=jnp.int32)[:, None], (blocks, slot_count))
    slot_ids = jnp.broadcast_to(jnp.arange(slot_count, dtype=jnp.int32)[None, :], (blocks, slot_count))
    table = jnp.zeros((blocks, EXPERTS * MOST), jnp.int32).at[block_ids, target].set(slot_ids)
    filled = jnp.zeros((blocks, EXPERTS * MOST), jnp.int32).at[block_ids, target].set(1)
    table = table.reshape(blocks, EXPERTS, MOST).transpose(1, 0, 2)
    filled = filled.reshape(blocks, EXPERTS, MOST).transpose(1, 0, 2)
    flat_weights = route_weights.reshape(-1)
    grad_scale = (tokens_all * TOP / EXPERTS) ** -0.5
    group_rows = blocks * MOST // N_DP
    row_blocks = jnp.repeat(jnp.arange(blocks, dtype=jnp.int32), MOST)

    def group_sum(left, right):
        left_f = left.astype(jnp.float32).reshape(N_DP, group_rows, -1)
        right_f = right.astype(jnp.float32).reshape(N_DP, group_rows, -1)
        parts = (grad_scale * jnp.einsum("grd,grf->gdf", left_f, right_f)).astype(jnp.bfloat16)
        return jnp.sum(parts.astype(jnp.float32), axis=0).astype(jnp.bfloat16)

    def step(carry, expert_id):
        dx_acc, prob_acc = carry
        slot_here = table[expert_id].reshape(-1)
        keep_here = filled[expert_id].reshape(-1)
        token_of = row_blocks * TOK_DEV + slot_here // TOP
        pick_of = slot_here % TOP
        keep_rows = keep_here.astype(inputs.dtype)[:, None]
        x_rows = inputs[token_of] * keep_rows
        dy_rows = masked[token_of] * keep_rows
        weight_rows = flat_weights[token_of * TOP + pick_of] * keep_here.astype(route_weights.dtype)
        w_gate = gate_weight[expert_id]
        w_up = up_weight[expert_id]
        w_down = down_weight[expert_id]
        gate_pre = jnp.dot(x_rows, w_gate, preferred_element_type=jnp.float32)
        up_pre = jnp.dot(x_rows, w_up, preferred_element_type=jnp.float32)
        activated, slope = silu_parts(gate_pre)
        hidden = (activated * up_pre).astype(jnp.bfloat16)
        raw_grad = jnp.dot(dy_rows, w_down.T, preferred_element_type=jnp.float32)
        prob_grad = jnp.sum(hidden.astype(jnp.float32) * raw_grad, axis=1).astype(jnp.bfloat16)
        weight_col = weight_rows.astype(jnp.float32)[:, None]
        scaled = (weight_col * dy_rows.astype(jnp.float32)).astype(jnp.bfloat16)
        pushed = weight_col * raw_grad
        d_gate = (pushed * up_pre * slope).astype(jnp.bfloat16)
        d_up = (pushed * activated).astype(jnp.bfloat16)
        slot_dx = (jnp.dot(d_gate, w_gate.T, preferred_element_type=jnp.float32)
                   + jnp.dot(d_up, w_up.T, preferred_element_type=jnp.float32)).astype(jnp.bfloat16)
        grad_gate = group_sum(x_rows, d_gate)
        grad_up = group_sum(x_rows, d_up)
        grad_down = group_sum(hidden, scaled)
        dx_acc = dx_acc.at[token_of].add(slot_dx.astype(jnp.float32) * keep_rows.astype(jnp.float32))
        prob_acc = prob_acc.at[token_of, pick_of].add(prob_grad.astype(jnp.float32) * keep_here.astype(jnp.float32))
        return (dx_acc, prob_acc), (grad_gate, grad_up, grad_down)

    start_state = (jnp.zeros((tokens_all, model_width), jnp.float32), jnp.zeros((tokens_all, TOP), jnp.float32))
    (dx_acc, prob_acc), (gate_grad, up_grad, down_grad) = lax.scan(step, start_state, jnp.arange(EXPERTS, dtype=jnp.int32))
    return dx_acc.astype(jnp.bfloat16), gate_grad, up_grad, down_grad, prob_acc.astype(jnp.bfloat16)
```

```python
import functools

import jax
import jax.numpy as jnp
from jax import lax
from jax.experimental import pallas as pl
from jax.experimental.pallas import tpu as pltpu
from jax.sharding import PartitionSpec as P

F32 = jnp.float32
BF16 = jnp.bfloat16
I32 = jnp.int32
CELL = 16
EXTRA = 2
SLABS = CELL // EXTRA
VMEM_LIMIT = 56 * 1024 * 1024


def iota(shape, dim):
    return lax.broadcasted_iota(I32, shape, dim)


def mm(a, b, ca=1, cb=0):
    return lax.dot_general(a, b, (((ca,), (cb,)), ((), ())), preferred_element_type=F32)


def cell_tables(routes_t, local, local_count, owners):
    top_k, tokens = routes_t.shape
    wanted = iota((owners, tokens), 0) * local_count + local
    names = jnp.zeros((owners, tokens), F32)
    for k in range(top_k):
        names = names + jnp.where(routes_t[k : k + 1, :] == wanted, 1.0, 0.0)
    before = jnp.where(iota((tokens, tokens), 0) < iota((tokens, tokens), 1), 1.0, 0.0)
    rank = mm(names.astype(BF16), before.astype(BF16))
    rank = jnp.where(names > 0.5, rank, -1.0)
    rows = owners * CELL
    spread = jnp.where(iota((rows, owners), 0) // CELL == iota((rows, owners), 1), 1.0, 0.0)
    spread = spread.astype(BF16)
    rank_rows = mm(spread, rank.astype(BF16)).astype(I32)
    place = iota((rows, tokens), 0) % CELL
    whole = rank_rows == place
    cut = rank_rows == CELL + place % EXTRA
    return wanted, spread, place, whole, cut


def pack_kernel(local, local_count, owners, routes_ref, weights_ref, count_ref, x_ref, dy_ref, out_ref):
    top_k, tokens = routes_ref.shape
    width = x_ref.shape[1]
    slab = width // SLABS
    routes_t = routes_ref[...]
    wanted, spread, place, whole, cut = cell_tables(routes_t, local, local_count, owners)
    combine = jnp.zeros((owners, tokens), F32)
    for k in range(top_k):
        combine = combine + jnp.where(
            routes_t[k : k + 1, :] == wanted, weights_ref[k : k + 1, :].astype(F32), 0.0
        )
    combine_rows = mm(spread, combine.astype(BF16))
    live = iota((1, tokens), 1) >= tokens - count_ref[0]
    pick_x = jnp.where(whole, 1.0, 0.0).astype(BF16)
    pick_dy = jnp.where(whole & live, 1.0, 0.0).astype(BF16)
    out_ref[:, :width] = mm(pick_x, x_ref[...]).astype(BF16)
    out_ref[:, width : 2 * width] = mm(pick_dy, dy_ref[...]).astype(BF16)
    cut_x, cut_dy = 0.0, 0.0
    for j in range(SLABS):
        here = cut & (place // EXTRA == j)
        columns = pl.ds(j * slab, slab)
        cut_x = cut_x + mm(jnp.where(here, 1.0, 0.0).astype(BF16), x_ref[:, columns])
        cut_dy = cut_dy + mm(jnp.where(here & live, 1.0, 0.0).astype(BF16), dy_ref[:, columns])
    out_ref[:, 2 * width : 2 * width + slab] = cut_x.astype(BF16)
    out_ref[:, 2 * width + slab : 2 * width + 2 * slab] = cut_dy.astype(BF16)
    whole_weight = jnp.sum(jnp.where(whole, combine_rows, 0.0), axis=1, keepdims=True)
    cut_weight = jnp.sum(jnp.where(cut, combine_rows, 0.0), axis=1, keepdims=True)
    lane = iota((owners * CELL, 128), 1)
    out_ref[:, 2 * width + 2 * slab :] = jnp.where(lane < 64, whole_weight, cut_weight).astype(BF16)


def expert_kernel(
    groups, grad_scale, recv_ref, wg_ref, wu_ref, wd_ref, grads_ref, back_ref,
    x_all, dy_all, gu_grad, hidden_all,
):
    rows = recv_ref.shape[0]
    width, units = wg_ref.shape
    owners = rows // CELL
    extra = owners * EXTRA
    total = rows + extra
    slab = width // SLABS
    r = iota((extra, rows), 1)
    q = iota((extra, rows), 0)
    x_all[:rows, :] = recv_ref[:, :width]
    dy_all[:rows, :] = recv_ref[:, width : 2 * width]
    cut_x = recv_ref[:, 2 * width : 2 * width + slab]
    cut_dy = recv_ref[:, 2 * width + slab : 2 * width + 2 * slab]
    weight_block = recv_ref[:, 2 * width + 2 * slab :]

    def joiner(j):
        source = q // EXTRA * CELL + j * EXTRA + q % EXTRA
        return jnp.where(r == source, 1.0, 0.0).astype(BF16)

    for j in range(SLABS):
        columns = pl.ds(j * slab, slab)
        x_all[rows:, columns] = mm(joiner(j), cut_x).astype(BF16)
        dy_all[rows:, columns] = mm(joiner(j), cut_dy).astype(BF16)
    weight_whole = weight_block[:, 0:1].astype(F32)
    weight_cut = mm(joiner(0), weight_block)[:, 64:65]
    weight = jnp.concatenate([weight_whole, weight_cut], axis=0)

    step = total // 3
    probs = []
    for i in range(3):
        here = pl.ds(i * step, step)
        x = x_all[here, :]
        dy = dy_all[here, :]
        gate_pre = mm(x, wg_ref[...])
        up_pre = mm(x, wu_ref[...])
        raw = mm(dy, wd_ref[...], 1, 1)
        sig = jax.nn.sigmoid(gate_pre)
        activated = gate_pre * sig
        slope = sig * (1.0 + gate_pre * (1.0 - sig))
        hidden = (activated * up_pre).astype(BF16)
        probs.append(jnp.sum(hidden.astype(F32) * raw, axis=1, keepdims=True))
        w = weight[i * step : (i + 1) * step, :]
        pushed = w * raw
        hidden_all[here, :] = hidden
        gu_grad[here, :units] = (pushed * up_pre * slope).astype(BF16)
        gu_grad[here, units:] = (pushed * activated).astype(BF16)
        dy_all[here, :] = (w * dy.astype(F32)).astype(BF16)

    part = width // groups
    block = grads_ref.shape[0] // groups
    side = grads_ref.shape[1]
    for g in range(groups):
        columns = pl.ds(g * part, part)
        gu = (grad_scale * mm(x_all[:, columns], gu_grad[...], 0, 0)).astype(BF16)
        for s in range(2 * units // side):
            grads_ref[pl.ds(g * block + s * part, part), :] = gu[:, s * side : (s + 1) * side]
        down = grad_scale * mm(hidden_all[...], dy_all[:, columns], 0, 0)
        grads_ref[pl.ds(g * block + 2 * units // side * part, units), :] = down.astype(BF16)

    prob = jnp.concatenate(probs, axis=0)
    cut_back = jnp.zeros((rows, slab), F32)
    r_t = iota((rows, extra), 0)
    q_t = iota((rows, extra), 1)
    half = rows // 2
    for i in range(2):
        here = pl.ds(i * half, half)
        dx = mm(gu_grad[here, :units], wg_ref[...], 1, 1) + mm(gu_grad[here, units:], wu_ref[...], 1, 1)
        back_ref[here, :width] = dx.astype(BF16)
    here = pl.ds(rows, extra)
    dx = mm(gu_grad[here, :units], wg_ref[...], 1, 1) + mm(gu_grad[here, units:], wu_ref[...], 1, 1)
    dx = dx.astype(BF16)
    for j in range(SLABS):
        source = q_t // EXTRA * CELL + j * EXTRA + q_t % EXTRA
        splitter = jnp.where(r_t == source, 1.0, 0.0).astype(BF16)
        cut_back = cut_back + mm(splitter, dx[:, j * slab : (j + 1) * slab])
    back_ref[:, width : width + slab] = cut_back.astype(BF16)
    same = (r_t // CELL == q_t // EXTRA) & (r_t % EXTRA == q_t % EXTRA)
    prob_cut = jnp.broadcast_to(prob[rows:, :], (extra, 128)).astype(BF16)
    prob_cut = mm(jnp.where(same, 1.0, 0.0).astype(BF16), prob_cut)
    lane = iota((rows, 128), 1)
    back_ref[:, width + slab :] = jnp.where(lane < 64, prob[:rows, :], prob_cut).astype(BF16)


def combine_kernel(local_count, owners, routes_ref, *refs):
    back_refs = refs[:local_count]
    dx_ref, prob_ref = refs[local_count:]
    top_k, tokens = routes_ref.shape
    width = dx_ref.shape[1]
    slab = width // SLABS
    routes_t = routes_ref[...]
    dx = 0.0
    cut_dx = [0.0] * SLABS
    probs = [0.0] * top_k
    for local in range(local_count):
        back_ref = back_refs[local]
        wanted, spread, place, whole, cut = cell_tables(routes_t, local, local_count, owners)
        dx = dx + mm(jnp.where(whole, 1.0, 0.0).astype(BF16), back_ref[:, :width], 0, 0)
        for j in range(SLABS):
            here = jnp.where(cut & (place // EXTRA == j), 1.0, 0.0).astype(BF16)
            cut_dx[j] = cut_dx[j] + mm(here, back_ref[:, width : width + slab], 0, 0)
        block = back_ref[:, width + slab :].astype(F32)
        held = jnp.where(whole, block[:, 0:1], 0.0)
        held = held + jnp.where(cut & (place // EXTRA == 0), block[:, 64:65], 0.0)
        by_owner = mm(spread, held.astype(BF16), 0, 0)
        for k in range(top_k):
            mine = jnp.where(routes_t[k : k + 1, :] == wanted, by_owner, 0.0)
            probs[k] = probs[k] + jnp.sum(mine, axis=0, keepdims=True)
    for j in range(SLABS):
        columns = slice(j * slab, (j + 1) * slab)
        dx_ref[:, columns] = (dx[:, columns] + cut_dx[j]).astype(BF16)
    for k in range(top_k):
        prob_ref[k : k + 1, :] = probs[k]


def vmem():
    return pl.BlockSpec(memory_space=pltpu.VMEM)


def shards(
    inputs, out_grad, route_weights, routes, response_counts, gate_weight, up_weight, down_weight
):
    tokens, width = inputs.shape
    top_k = routes.shape[1]
    local_count, _, units = gate_weight.shape
    owners = lax.axis_size("expert")
    groups = lax.axis_size("dp")
    grad_scale = (tokens * top_k * groups / local_count) ** (-0.5)
    rows = owners * CELL
    extra = owners * EXTRA
    slab = width // SLABS
    send_width = 2 * width + 2 * slab + 128
    back_width = width + slab + 128
    part = width // groups
    block = (2 * units * part + units * part) // part
    params = pltpu.CompilerParams(vmem_limit_bytes=VMEM_LIMIT)
    routes_t = routes.T
    weights_t = route_weights.T

    def exchange(array):
        cols = array.shape[1]
        return lax.all_to_all(
            array.reshape(owners, CELL, cols), "expert", split_axis=0, concat_axis=0, tiled=True
        ).reshape(rows, cols)

    received = []
    for local in range(local_count):
        packed = pl.pallas_call(
            functools.partial(pack_kernel, local, local_count, owners),
            out_shape=jax.ShapeDtypeStruct((rows, send_width), BF16),
            in_specs=[vmem(), vmem(), pl.BlockSpec(memory_space=pltpu.SMEM), vmem(), vmem()],
            out_specs=vmem(),
            compiler_params=params,
            cost_estimate=pl.CostEstimate(
                flops=4 * rows * tokens * width, bytes_accessed=2 * rows * send_width, transcendentals=0
            ),
            name="pack",
        )(routes_t, weights_t, response_counts, inputs, out_grad)
        received.append(exchange(packed))

    sums, backs = [], []
    for local in range(local_count):
        grads, back = pl.pallas_call(
            functools.partial(expert_kernel, groups, grad_scale),
            out_shape=(
                jax.ShapeDtypeStruct((groups * 3 * units * part // part, part), BF16),
                jax.ShapeDtypeStruct((rows, back_width), BF16),
            ),
            in_specs=[vmem()] * 4,
            out_specs=(vmem(), vmem()),
            scratch_shapes=[
                pltpu.VMEM((rows + extra, width), BF16),
                pltpu.VMEM((rows + extra, width), BF16),
                pltpu.VMEM((rows + extra, 2 * units), BF16),
                pltpu.VMEM((rows + extra, units), BF16),
            ],
            compiler_params=params,
            cost_estimate=pl.CostEstimate(
                flops=16 * (rows + extra) * width * units,
                bytes_accessed=2 * rows * (send_width + back_width) + 12 * width * units,
                transcendentals=(rows + extra) * units,
            ),
            name="expert",
        )(received[local], gate_weight[local], up_weight[local], down_weight[local])
        backs.append(exchange(back))
        sums.append(lax.psum_scatter(grads, "dp", scatter_dimension=0, tiled=True))

    in_grad, prob_t = pl.pallas_call(
        functools.partial(combine_kernel, local_count, owners),
        out_shape=(
            jax.ShapeDtypeStruct((tokens, width), BF16),
            jax.ShapeDtypeStruct((top_k, tokens), F32),
        ),
        in_specs=[vmem()] * (1 + local_count),
        out_specs=(vmem(), vmem()),
        compiler_params=params,
        cost_estimate=pl.CostEstimate(
            flops=4 * rows * tokens * width, bytes_accessed=4 * rows * back_width, transcendentals=0
        ),
        name="combine",
    )(routes_t, *backs)
    route_weight_grad = prob_t.T.astype(BF16)

    gate_grad, up_grad, down_grad = [], [], []
    for total in sums:
        side = total.shape[1]
        pieces = 2 * units // side
        gu = jnp.concatenate([total[s * part : (s + 1) * part] for s in range(pieces)], axis=1)
        gate_grad.append(gu[:, :units])
        up_grad.append(gu[:, units:])
        down_grad.append(total[pieces * part :])
    return (
        in_grad,
        jnp.stack(gate_grad),
        jnp.stack(up_grad),
        jnp.stack(down_grad),
        route_weight_grad,
    )


def solution(mesh):
    tokens = P(("dp", "expert"), None)
    return jax.shard_map(
        shards,
        mesh=mesh,
        in_specs=(
            tokens, tokens, tokens, tokens,
            P(("dp", "expert")),
            P("expert", None, None), P("expert", None, None), P("expert", None, None),
        ),
        out_specs=(
            tokens, P("expert", "dp", None), P("expert", "dp", None), P("expert", None, "dp"), tokens,
        ),
        check_vma=False,
    )
```

```python
import functools

import jax
import jax.numpy as jnp
from jax import lax
from jax.experimental import pallas as pl
from jax.experimental.pallas import tpu as pltpu
from jax.sharding import PartitionSpec as P

F32 = jnp.float32
BF16 = jnp.bfloat16
I32 = jnp.int32
CELL = 16
EXTRA = 2
SLABS = CELL // EXTRA
VMEM_LIMIT = 60 * 1024 * 1024
MESH = pl.DeviceIdType.MESH


def iota(shape, dim):
    return lax.broadcasted_iota(I32, shape, dim)


def mm(a, b, ca=1, cb=0):
    return lax.dot_general(a, b, (((ca,), (cb,)), ((), ())), preferred_element_type=F32)


def cell_tables(routes_t, local, local_count, owners):
    top_k, tokens = routes_t.shape
    wanted = iota((owners, tokens), 0) * local_count + local
    names = jnp.zeros((owners, tokens), F32)
    for k in range(top_k):
        names = names + jnp.where(routes_t[k : k + 1, :] == wanted, 1.0, 0.0)
    before = jnp.where(iota((tokens, tokens), 0) < iota((tokens, tokens), 1), 1.0, 0.0)
    rank = mm(names.astype(BF16), before.astype(BF16))
    rank = jnp.where(names > 0.5, rank, -1.0)
    rows = owners * CELL
    spread = jnp.where(iota((rows, owners), 0) // CELL == iota((rows, owners), 1), 1.0, 0.0)
    spread = spread.astype(BF16)
    rank_rows = mm(spread, rank.astype(BF16)).astype(I32)
    place = iota((rows, tokens), 0) % CELL
    whole = rank_rows == place
    cut = rank_rows == CELL + place % EXTRA
    return wanted, spread, place, whole, cut


def pack(local, local_count, owners, routes_ref, weights_ref, count_ref, x_ref, dy_ref, out_ref):
    top_k, tokens = routes_ref.shape
    width = x_ref.shape[1]
    slab = width // SLABS
    routes_t = routes_ref[...]
    wanted, spread, place, whole, cut = cell_tables(routes_t, local, local_count, owners)
    combine = jnp.zeros((owners, tokens), F32)
    for k in range(top_k):
        combine = combine + jnp.where(
            routes_t[k : k + 1, :] == wanted, weights_ref[k : k + 1, :].astype(F32), 0.0
        )
    combine_rows = mm(spread, combine.astype(BF16))
    live = iota((1, tokens), 1) >= tokens - count_ref[0]
    pick_x = jnp.where(whole, 1.0, 0.0).astype(BF16)
    pick_dy = jnp.where(whole & live, 1.0, 0.0).astype(BF16)
    out_ref[:, :width] = mm(pick_x, x_ref[...]).astype(BF16)
    out_ref[:, width : 2 * width] = mm(pick_dy, dy_ref[...]).astype(BF16)
    cut_x, cut_dy = 0.0, 0.0
    for j in range(SLABS):
        here = cut & (place // EXTRA == j)
        columns = pl.ds(j * slab, slab)
        cut_x = cut_x + mm(jnp.where(here, 1.0, 0.0).astype(BF16), x_ref[:, columns])
        cut_dy = cut_dy + mm(jnp.where(here & live, 1.0, 0.0).astype(BF16), dy_ref[:, columns])
    out_ref[:, 2 * width : 2 * width + slab] = cut_x.astype(BF16)
    out_ref[:, 2 * width + slab : 2 * width + 2 * slab] = cut_dy.astype(BF16)
    whole_weight = jnp.sum(jnp.where(whole, combine_rows, 0.0), axis=1, keepdims=True)
    cut_weight = jnp.sum(jnp.where(cut, combine_rows, 0.0), axis=1, keepdims=True)
    lane = iota((owners * CELL, 128), 1)
    out_ref[:, 2 * width + 2 * slab :] = jnp.where(lane < 64, whole_weight, cut_weight).astype(BF16)


def whole_kernel(
    grad_scale,
    routes_ref, weights_ref, count_ref, x_ref, dy_ref, wg_ref, wu_ref, wd_ref,
    dx_ref, prob_ref, sums_ref, recv_ref,
    send, x_all, dy_all, side, gu_grad, hidden_all, w_gu, w_down, grads, flow_r, flow_l,
    back_send, back_recv,
    load_sem, own_sem, send_sem, recv_sem, back_own_sem, back_send_sem, back_recv_sem,
    weight_sem, flow_send_sem, flow_recv_sem,
):
    owners, groups = lax.axis_size("expert"), lax.axis_size("dp")
    me, z = lax.axis_index("expert"), lax.axis_index("dp")
    local_count, width, units = wg_ref.shape
    top_k, tokens = routes_ref.shape
    rows = owners * CELL
    extra = owners * EXTRA
    total = rows + extra
    slab = width // SLABS
    half = groups // 2
    block = grads.shape[2]
    top = block // 2
    ring_right = (lax.rem(z + 1, groups), me)
    ring_left = (lax.rem(z + groups - 1, groups), me)
    beside = (z, lax.rem(me + 1, owners))

    def load_weights(local, start):
        copies = [
            pltpu.make_async_copy(wg_ref.at[local], w_gu.at[:, pl.ds(0, units)], weight_sem.at[0]),
            pltpu.make_async_copy(wu_ref.at[local], w_gu.at[:, pl.ds(units, units)], weight_sem.at[1]),
            pltpu.make_async_copy(wd_ref.at[local], w_down, weight_sem.at[2]),
        ]
        for copy in copies:
            if start:
                copy.start()
            else:
                copy.wait()

    def spread_out(source, target, own, sends, recvs, local):
        pltpu.make_async_copy(
            source.at[local, pl.ds(me * CELL, CELL)], target.at[local, pl.ds(me * CELL, CELL)],
            own.at[local],
        ).start()

        def one(i, carry):
            to = lax.rem(me + i, owners)
            pltpu.make_async_remote_copy(
                src_ref=source.at[local, pl.ds(to * CELL, CELL)],
                dst_ref=target.at[local, pl.ds(me * CELL, CELL)],
                send_sem=sends.at[local],
                recv_sem=recvs.at[local],
                device_id=(z, to),
                device_id_type=MESH,
            ).start()
            return carry

        lax.fori_loop(1, owners, one, 0)

    def all_of(source, target, sends, recvs, local):
        most = pl.ds(0, rows - CELL)
        return pltpu.make_async_remote_copy(
            src_ref=source.at[local, most], dst_ref=target.at[local, most],
            send_sem=sends.at[local], recv_sem=recvs.at[local],
            device_id=beside, device_id_type=MESH,
        )

    def wait_own(source, target, own, local):
        pltpu.make_async_copy(
            source.at[local, pl.ds(me * CELL, CELL)], target.at[local, pl.ds(me * CELL, CELL)],
            own.at[local],
        ).wait()

    def hop(local, step, right):
        flow = flow_r if right else flow_l
        way = 0 if right else 1
        if step == 0:
            target = lax.rem(z + (half if right else groups - half), groups)
            part = pl.ds(0 if right else top, top)
            source, landing = grads.at[local, target, part], flow.at[local, 0, part]
        else:
            source, landing = flow.at[local, step - 1], flow.at[local, step]
        return pltpu.make_async_remote_copy(
            src_ref=source, dst_ref=landing,
            send_sem=flow_send_sem.at[local, way, step], recv_sem=flow_recv_sem.at[local, way, step],
            device_id=ring_right if right else ring_left, device_id_type=MESH,
        )

    def add_rows(out, terms):
        count = terms[0].shape[0]
        piece = count // 4

        def one(i, carry):
            here = pl.ds(pl.multiple_of(i * piece, piece), piece)
            value = terms[0][here, :].astype(F32)
            for term in terms[1:]:
                value = value + term[here, :].astype(F32)
            out[here, :] = value.astype(BF16)
            return carry

        lax.fori_loop(0, 4, one, 0)

    def ring_step(local, step):
        for right in (True, False):
            flow = flow_r if right else flow_l
            if step > 0:
                hop(local, step - 1, right).wait_recv()
                away = half - step
                target = lax.rem(z + (away if right else groups - away), groups)
                if step == 1:
                    fresh, rest = (0, top) if right else (top, 0)
                    here, there = pl.ds(fresh, top), pl.ds(rest, top)
                    held = flow.at[local, 0, here]
                    add_rows(held, [held, grads.at[local, target, here]])
                    flow[local, 0, there] = grads[local, target, there]
                else:
                    held = flow.at[local, step - 1]
                    add_rows(held, [held, grads.at[local, target]])
            hop(local, step, right).start()

    def ring_end(local):
        hop(local, half - 1, True).wait_recv()
        hop(local, half - 1, False).wait_recv()
        if half == 1:
            a, b = pl.ds(0, top), pl.ds(top, top)
            add_rows(sums_ref.at[local, a], [grads.at[local, z, a], flow_r.at[local, 0, a]])
            add_rows(sums_ref.at[local, b], [grads.at[local, z, b], flow_l.at[local, 0, b]])
        else:
            last = half - 1
            add_rows(
                sums_ref.at[local],
                [grads.at[local, z], flow_r.at[local, last], flow_l.at[local, last]],
            )

    r = iota((extra, rows), 1)
    q = iota((extra, rows), 0)
    r_t = iota((rows, extra), 0)
    q_t = iota((rows, extra), 1)

    def load_rows(local):
        all_of(send, recv_ref, send_sem, recv_sem, local).wait_recv()
        wait_own(send, recv_ref, own_sem, local)
        copies = [
            pltpu.make_async_copy(
                recv_ref.at[local, :, pl.ds(0, width)], x_all.at[pl.ds(0, rows)], load_sem.at[0]),
            pltpu.make_async_copy(
                recv_ref.at[local, :, pl.ds(width, width)], dy_all.at[pl.ds(0, rows)], load_sem.at[1]),
            pltpu.make_async_copy(
                recv_ref.at[local, :, pl.ds(2 * width, 2 * slab + 128)], side, load_sem.at[2]),
        ]
        for copy in copies:
            copy.start()
        for copy in copies:
            copy.wait()

    def forward(local):
        cut_x, cut_dy, weight_block = side[:, :slab], side[:, slab : 2 * slab], side[:, 2 * slab :]

        def joiner(j):
            source = q // EXTRA * CELL + j * EXTRA + q % EXTRA
            return jnp.where(r == source, 1.0, 0.0).astype(BF16)

        for j in range(SLABS):
            columns = pl.ds(j * slab, slab)
            x_all[rows:, columns] = mm(joiner(j), cut_x).astype(BF16)
            dy_all[rows:, columns] = mm(joiner(j), cut_dy).astype(BF16)
        weight_whole = weight_block[:, 0:1].astype(F32)
        weight_cut = mm(joiner(0), weight_block)[:, 64:65]
        weight = jnp.concatenate([weight_whole, weight_cut], axis=0)
        step = total // 3
        probs = []
        for i in range(3):
            here = pl.ds(i * step, step)
            dy = dy_all[here, :]
            pre = mm(x_all[here, :], w_gu[...])
            gate_pre, up_pre = pre[:, :units], pre[:, units:]
            raw = mm(dy, w_down[...], 1, 1)
            sig = jax.nn.sigmoid(gate_pre)
            activated = gate_pre * sig
            slope = sig * (1.0 + gate_pre * (1.0 - sig))
            hidden = (activated * up_pre).astype(BF16)
            probs.append(jnp.sum(hidden.astype(F32) * raw, axis=1, keepdims=True))
            w = weight[i * step : (i + 1) * step, :]
            pushed = w * raw
            hidden_all[here, :] = hidden
            gu_grad[here, :units] = (pushed * up_pre * slope).astype(BF16)
            gu_grad[here, units:] = (pushed * activated).astype(BF16)
            dy_all[here, :] = (w * dy.astype(F32)).astype(BF16)
        prob = jnp.concatenate(probs, axis=0)
        same = (r_t // CELL == q_t // EXTRA) & (r_t % EXTRA == q_t % EXTRA)
        prob_cut = jnp.broadcast_to(prob[rows:, :], (extra, 128)).astype(BF16)
        prob_cut = mm(jnp.where(same, 1.0, 0.0).astype(BF16), prob_cut)
        lane = iota((rows, 128), 1)
        back_send[local, :, width + slab :] = jnp.where(lane < 64, prob[:rows, :], prob_cut).astype(BF16)

    def weight_grads(local):
        part = width // groups
        pieces = 2 * units // part

        def one(g, carry):
            columns = pl.ds(pl.multiple_of(g * part, part), part)
            gu = (grad_scale * mm(x_all[:, columns], gu_grad[...], 0, 0)).astype(BF16)
            for s in range(pieces):
                grads[local, g, s * part : (s + 1) * part, :] = gu[:, s * part : (s + 1) * part]
            down = grad_scale * mm(hidden_all[...], dy_all[:, columns], 0, 0)
            grads[local, g, pieces * part :, :] = down.astype(BF16)
            return carry

        lax.fori_loop(0, groups, one, 0)

    def input_grads(local):
        piece = rows // 2
        for i in range(2):
            here = pl.ds(i * piece, piece)
            back_send[local, here, :width] = mm(gu_grad[here, :], w_gu[...], 1, 1).astype(BF16)
        dx = mm(gu_grad[rows:, :], w_gu[...], 1, 1).astype(BF16)
        cut_back = 0.0
        for j in range(SLABS):
            source = q_t // EXTRA * CELL + j * EXTRA + q_t % EXTRA
            splitter = jnp.where(r_t == source, 1.0, 0.0).astype(BF16)
            cut_back = cut_back + mm(splitter, dx[:, j * slab : (j + 1) * slab])
        back_send[local, :, width : width + slab] = cut_back.astype(BF16)

    load_weights(0, True)
    barrier = pltpu.get_barrier_semaphore()

    def greet(i, carry):
        pl.semaphore_signal(barrier, inc=1, device_id=(z, lax.rem(me + i, owners)), device_id_type=MESH)
        return carry

    lax.fori_loop(1, owners, greet, 0)
    pl.semaphore_signal(barrier, inc=1, device_id=ring_right, device_id_type=MESH)
    pl.semaphore_signal(barrier, inc=1, device_id=ring_left, device_id_type=MESH)
    pack(0, local_count, owners, routes_ref, weights_ref, count_ref, x_ref, dy_ref, send.at[0])
    pl.semaphore_wait(barrier, owners + 1)
    spread_out(send, recv_ref, own_sem, send_sem, recv_sem, 0)
    pack(1, local_count, owners, routes_ref, weights_ref, count_ref, x_ref, dy_ref, send.at[1])
    all_of(send, recv_ref, send_sem, recv_sem, 0).wait_send()
    spread_out(send, recv_ref, own_sem, send_sem, recv_sem, 1)

    load_weights(0, False)
    load_rows(0)
    forward(0)
    weight_grads(0)
    ring_step(0, 0)
    input_grads(0)
    spread_out(back_send, back_recv, back_own_sem, back_send_sem, back_recv_sem, 0)
    load_weights(1, True)
    for step in range(1, half):
        ring_step(0, step)

    load_weights(1, False)
    load_rows(1)
    forward(1)
    weight_grads(1)
    ring_step(1, 0)
    input_grads(1)
    spread_out(back_send, back_recv, back_own_sem, back_send_sem, back_recv_sem, 1)
    ring_end(0)
    for step in range(1, half):
        ring_step(1, step)
    for local in range(local_count):
        all_of(back_send, back_recv, back_send_sem, back_recv_sem, local).wait_recv()
        wait_own(back_send, back_recv, back_own_sem, local)
    combine(local_count, owners, routes_ref, [back_recv.at[i] for i in range(local_count)], dx_ref, prob_ref)
    ring_end(1)
    all_of(send, recv_ref, send_sem, recv_sem, 1).wait_send()
    for local in range(local_count):
        all_of(back_send, back_recv, back_send_sem, back_recv_sem, local).wait_send()
        for step in range(half):
            hop(local, step, True).wait_send()
            hop(local, step, False).wait_send()


def combine(local_count, owners, routes_ref, back_refs, dx_ref, prob_ref):
    top_k, tokens = routes_ref.shape
    width = dx_ref.shape[1]
    slab = width // SLABS
    routes_t = routes_ref[...]
    dx = 0.0
    cut_dx = [0.0] * SLABS
    probs = [0.0] * top_k
    for local in range(local_count):
        back_ref = back_refs[local]
        wanted, spread, place, whole, cut = cell_tables(routes_t, local, local_count, owners)
        dx = dx + mm(jnp.where(whole, 1.0, 0.0).astype(BF16), back_ref[:, :width], 0, 0)
        for j in range(SLABS):
            here = jnp.where(cut & (place // EXTRA == j), 1.0, 0.0).astype(BF16)
            cut_dx[j] = cut_dx[j] + mm(here, back_ref[:, width : width + slab], 0, 0)
        block = back_ref[:, width + slab :].astype(F32)
        held = jnp.where(whole, block[:, 0:1], 0.0)
        held = held + jnp.where(cut & (place // EXTRA == 0), block[:, 64:65], 0.0)
        by_owner = mm(spread, held.astype(BF16), 0, 0)
        for k in range(top_k):
            mine = jnp.where(routes_t[k : k + 1, :] == wanted, by_owner, 0.0)
            probs[k] = probs[k] + jnp.sum(mine, axis=0, keepdims=True)
    for j in range(SLABS):
        columns = slice(j * slab, (j + 1) * slab)
        dx_ref[:, columns] = (dx[:, columns] + cut_dx[j]).astype(BF16)
    for k in range(top_k):
        prob_ref[k : k + 1, :] = probs[k]


def vmem():
    return pl.BlockSpec(memory_space=pltpu.VMEM)


def shards(
    inputs, out_grad, route_weights, routes, response_counts, gate_weight, up_weight, down_weight
):
    tokens, width = inputs.shape
    top_k = routes.shape[1]
    local_count, _, units = gate_weight.shape
    owners = lax.axis_size("expert")
    groups = lax.axis_size("dp")
    grad_scale = (tokens * top_k * groups / local_count) ** (-0.5)
    rows = owners * CELL
    extra = owners * EXTRA
    slab = width // SLABS
    half = groups // 2
    send_width = 2 * width + 2 * slab + 128
    back_width = width + slab + 128
    part = width // groups
    block = 3 * units
    dma = pltpu.SemaphoreType.DMA
    in_grad, prob_t, sums, _ = pl.pallas_call(
        functools.partial(whole_kernel, grad_scale),
        out_shape=(
            jax.ShapeDtypeStruct((tokens, width), BF16),
            jax.ShapeDtypeStruct((top_k, tokens), F32),
            jax.ShapeDtypeStruct((local_count, block, part), BF16),
            jax.ShapeDtypeStruct((local_count, rows, send_width), BF16),
        ),
        in_specs=[vmem(), vmem(), pl.BlockSpec(memory_space=pltpu.SMEM), vmem(), vmem()]
        + [pl.BlockSpec(memory_space=pl.ANY)] * 3,
        out_specs=(vmem(), vmem(), vmem(), pl.BlockSpec(memory_space=pl.ANY)),
        scratch_shapes=[
            pltpu.VMEM((local_count, rows, send_width), BF16),
            pltpu.VMEM((rows + extra, width), BF16),
            pltpu.VMEM((rows + extra, width), BF16),
            pltpu.VMEM((rows, 2 * slab + 128), BF16),
            pltpu.VMEM((rows + extra, 2 * units), BF16),
            pltpu.VMEM((rows + extra, units), BF16),
            pltpu.VMEM((width, 2 * units), BF16),
            pltpu.VMEM((units, width), BF16),
            pltpu.VMEM((local_count, groups, block, part), BF16),
            pltpu.VMEM((local_count, half, block, part), BF16),
            pltpu.VMEM((local_count, half, block, part), BF16),
            pltpu.VMEM((local_count, rows, back_width), BF16),
            pltpu.VMEM((local_count, rows, back_width), BF16),
            dma((3,)), dma((2,)), dma((2,)), dma((2,)), dma((2,)), dma((2,)), dma((2,)),
            dma((3,)), dma((2, 2, half)), dma((2, 2, half)),
        ],
        compiler_params=pltpu.CompilerParams(
            vmem_limit_bytes=VMEM_LIMIT, collective_id=0, has_side_effects=True
        ),
        name="whole",
    )(routes.T, route_weights.T, response_counts, inputs, out_grad, gate_weight, up_weight, down_weight)
    route_weight_grad = prob_t.T.astype(BF16)

    gate_grad, up_grad, down_grad = [], [], []
    for local in range(local_count):
        total = sums[local]
        side = total.shape[1]
        pieces = 2 * units // side
        gu = jnp.concatenate([total[s * part : (s + 1) * part] for s in range(pieces)], axis=1)
        gate_grad.append(gu[:, :units])
        up_grad.append(gu[:, units:])
        down_grad.append(total[pieces * part :])
    return (
        in_grad,
        jnp.stack(gate_grad),
        jnp.stack(up_grad),
        jnp.stack(down_grad),
        route_weight_grad,
    )


def solution(mesh):
    tokens = P(("dp", "expert"), None)
    return jax.shard_map(
        shards,
        mesh=mesh,
        in_specs=(
            tokens, tokens, tokens, tokens,
            P(("dp", "expert")),
            P("expert", None, None), P("expert", None, None), P("expert", None, None),
        ),
        out_specs=(
            tokens, P("expert", "dp", None), P("expert", "dp", None), P("expert", None, "dp"), tokens,
        ),
        check_vma=False,
    )
```

```python
import functools

import jax
import jax.numpy as jnp
from jax import lax
from jax.experimental import pallas as pl
from jax.experimental.pallas import tpu as pltpu
from jax.sharding import PartitionSpec as P

F32 = jnp.float32
BF16 = jnp.bfloat16
I32 = jnp.int32
CELL = 16
EXTRA = 2
SLABS = CELL // EXTRA
VMEM_LIMIT = 60 * 1024 * 1024
MESH = pl.DeviceIdType.MESH


def iota(shape, dim):
    return lax.broadcasted_iota(I32, shape, dim)


def mm(a, b, ca=1, cb=0):
    return lax.dot_general(a, b, (((ca,), (cb,)), ((), ())), preferred_element_type=F32)


def cell_tables(routes_t, local, local_count, owners):
    top_k, tokens = routes_t.shape
    wanted = iota((owners, tokens), 0) * local_count + local
    names = jnp.zeros((owners, tokens), F32)
    for k in range(top_k):
        names = names + jnp.where(routes_t[k : k + 1, :] == wanted, 1.0, 0.0)
    before = jnp.where(iota((tokens, tokens), 0) < iota((tokens, tokens), 1), 1.0, 0.0)
    rank = mm(names.astype(BF16), before.astype(BF16))
    rank = jnp.where(names > 0.5, rank, -1.0)
    rows = owners * CELL
    spread = jnp.where(iota((rows, owners), 0) // CELL == iota((rows, owners), 1), 1.0, 0.0)
    spread = spread.astype(BF16)
    rank_rows = mm(spread, rank.astype(BF16)).astype(I32)
    place = iota((rows, tokens), 0) % CELL
    whole = rank_rows == place
    cut = rank_rows == CELL + place % EXTRA
    return wanted, spread, place, whole, cut


def pack(local, local_count, owners, routes_ref, weights_ref, count_ref, x_ref, dy_ref, out_ref):
    top_k, tokens = routes_ref.shape
    width = x_ref.shape[1]
    slab = width // SLABS
    routes_t = routes_ref[...]
    wanted, spread, place, whole, cut = cell_tables(routes_t, local, local_count, owners)
    combine = jnp.zeros((owners, tokens), F32)
    for k in range(top_k):
        combine = combine + jnp.where(
            routes_t[k : k + 1, :] == wanted, weights_ref[k : k + 1, :].astype(F32), 0.0
        )
    combine_rows = mm(spread, combine.astype(BF16))
    live = iota((1, tokens), 1) >= tokens - count_ref[0]
    pick_x = jnp.where(whole, 1.0, 0.0).astype(BF16)
    pick_dy = jnp.where(whole & live, 1.0, 0.0).astype(BF16)
    out_ref[:, :width] = mm(pick_x, x_ref[...]).astype(BF16)
    out_ref[:, width : 2 * width] = mm(pick_dy, dy_ref[...]).astype(BF16)
    cut_x, cut_dy = 0.0, 0.0
    for j in range(SLABS):
        here = cut & (place // EXTRA == j)
        columns = pl.ds(j * slab, slab)
        cut_x = cut_x + mm(jnp.where(here, 1.0, 0.0).astype(BF16), x_ref[:, columns])
        cut_dy = cut_dy + mm(jnp.where(here & live, 1.0, 0.0).astype(BF16), dy_ref[:, columns])
    out_ref[:, 2 * width : 2 * width + slab] = cut_x.astype(BF16)
    out_ref[:, 2 * width + slab : 2 * width + 2 * slab] = cut_dy.astype(BF16)
    whole_weight = jnp.sum(jnp.where(whole, combine_rows, 0.0), axis=1, keepdims=True)
    cut_weight = jnp.sum(jnp.where(cut, combine_rows, 0.0), axis=1, keepdims=True)
    lane = iota((owners * CELL, 128), 1)
    out_ref[:, 2 * width + 2 * slab :] = jnp.where(lane < 64, whole_weight, cut_weight).astype(BF16)


def whole_kernel(
    grad_scale,
    routes_ref, weights_ref, count_ref, x_ref, dy_ref, wg_ref, wu_ref, wd_ref,
    dx_ref, prob_ref, gate_ref, up_ref, down_ref, recv_ref,
    send, x_all, dy_all, side, gu_grad, hidden_all, w_gu, w_down, grads, flow_r, flow_l,
    back_send, back_recv,
    load_sem, own_sem, send_sem, recv_sem, back_own_sem, back_send_sem, back_recv_sem,
    weight_sem, flow_send_sem, flow_recv_sem,
):
    owners, groups = lax.axis_size("expert"), lax.axis_size("dp")
    me, z = lax.axis_index("expert"), lax.axis_index("dp")
    local_count, width, units = wg_ref.shape
    top_k, tokens = routes_ref.shape
    rows = owners * CELL
    extra = owners * EXTRA
    total = rows + extra
    slab = width // SLABS
    half = groups // 2
    block = grads.shape[2]
    top = block // 2
    ring_right = (lax.rem(z + 1, groups), me)
    ring_left = (lax.rem(z + groups - 1, groups), me)
    beside = (z, lax.rem(me + 1, owners))

    def load_weights(local, start):
        copies = [
            pltpu.make_async_copy(wg_ref.at[local], w_gu.at[:, pl.ds(0, units)], weight_sem.at[0]),
            pltpu.make_async_copy(wu_ref.at[local], w_gu.at[:, pl.ds(units, units)], weight_sem.at[1]),
            pltpu.make_async_copy(wd_ref.at[local], w_down, weight_sem.at[2]),
        ]
        for copy in copies:
            if start:
                copy.start()
            else:
                copy.wait()

    def spread_out(source, target, own, sends, recvs, local):
        pltpu.make_async_copy(
            source.at[local, pl.ds(me * CELL, CELL)], target.at[local, pl.ds(me * CELL, CELL)],
            own.at[local],
        ).start()

        tiles = source.shape[2] // 128
        pieces = max(1, tiles // 4)
        for c in range(pieces):
            low, high = tiles * c // pieces * 128, tiles * (c + 1) // pieces * 128

            def one(i, carry, columns=pl.ds(low, high - low)):
                to = lax.rem(me + i, owners)
                pltpu.make_async_remote_copy(
                    src_ref=source.at[local, pl.ds(to * CELL, CELL), columns],
                    dst_ref=target.at[local, pl.ds(me * CELL, CELL), columns],
                    send_sem=sends.at[local],
                    recv_sem=recvs.at[local],
                    device_id=(z, to),
                    device_id_type=MESH,
                ).start()
                return carry

            lax.fori_loop(1, owners, one, 0)

    def all_of(source, target, sends, recvs, local):
        most = pl.ds(0, rows - CELL)
        return pltpu.make_async_remote_copy(
            src_ref=source.at[local, most], dst_ref=target.at[local, most],
            send_sem=sends.at[local], recv_sem=recvs.at[local],
            device_id=beside, device_id_type=MESH,
        )

    def wait_own(source, target, own, local):
        pltpu.make_async_copy(
            source.at[local, pl.ds(me * CELL, CELL)], target.at[local, pl.ds(me * CELL, CELL)],
            own.at[local],
        ).wait()

    def hop(local, step, right):
        flow = flow_r if right else flow_l
        way = 0 if right else 1
        if step == 0:
            target = lax.rem(z + (half if right else groups - half), groups)
            part = pl.ds(0 if right else top, top)
            source, landing = grads.at[local, target, part], flow.at[local, 0, part]
        else:
            source, landing = flow.at[local, step - 1], flow.at[local, step]
        return pltpu.make_async_remote_copy(
            src_ref=source, dst_ref=landing,
            send_sem=flow_send_sem.at[local, way, step], recv_sem=flow_recv_sem.at[local, way, step],
            device_id=ring_right if right else ring_left, device_id_type=MESH,
        )

    def add_rows(out, terms):
        count = terms[0].shape[0]
        piece = count // 4

        def one(i, carry):
            here = pl.ds(pl.multiple_of(i * piece, piece), piece)
            value = terms[0][here, :].astype(F32)
            for term in terms[1:]:
                value = value + term[here, :].astype(F32)
            out[here, :] = value.astype(BF16)
            return carry

        lax.fori_loop(0, 4, one, 0)

    def ring_step(local, step):
        for right in (True, False):
            flow = flow_r if right else flow_l
            if step > 0:
                hop(local, step - 1, right).wait_recv()
                away = half - step
                target = lax.rem(z + (away if right else groups - away), groups)
                if step == 1:
                    fresh, rest = (0, top) if right else (top, 0)
                    here, there = pl.ds(fresh, top), pl.ds(rest, top)
                    held = flow.at[local, 0, here]
                    add_rows(held, [held, grads.at[local, target, here]])
                    flow[local, 0, there] = grads[local, target, there]
                else:
                    held = flow.at[local, step - 1]
                    add_rows(held, [held, grads.at[local, target]])
            hop(local, step, right).start()

    def ring_end(local):
        last = half - 1
        hop(local, last, True).wait_recv()
        hop(local, last, False).wait_recv()
        part = width // groups
        pieces = 2 * units // part

        def summed(low, count):
            here = pl.ds(low, count)
            value = grads[local, z, here, :].astype(F32)
            if half > 1 or low < top:
                value = value + flow_r[local, last, here, :].astype(F32)
            if half > 1 or low >= top:
                value = value + flow_l[local, last, here, :].astype(F32)
            return value.astype(BF16)

        step = part // 2
        for i in range(2 * pieces):
            value = summed(i * step, step)
            at, here = i // 2 * part, slice(i % 2 * step, (i % 2 + 1) * step)
            in_gate = max(0, min(part, units - at))
            if in_gate > 0:
                gate_ref[local, here, at : at + in_gate] = value[:, :in_gate]
            if in_gate < part:
                up_ref[local, here, at + in_gate - units : at + part - units] = value[:, in_gate:]
        for i in range(units // step):
            down_ref[local, i * step : (i + 1) * step, :] = summed(pieces * part + i * step, step)

    r = iota((extra, rows), 1)
    q = iota((extra, rows), 0)
    r_t = iota((rows, extra), 0)
    q_t = iota((rows, extra), 1)

    def load_rows(local):
        all_of(send, recv_ref, send_sem, recv_sem, local).wait_recv()
        wait_own(send, recv_ref, own_sem, local)
        copies = [
            pltpu.make_async_copy(
                recv_ref.at[local, :, pl.ds(0, width)], x_all.at[pl.ds(0, rows)], load_sem.at[0]),
            pltpu.make_async_copy(
                recv_ref.at[local, :, pl.ds(width, width)], dy_all.at[pl.ds(0, rows)], load_sem.at[1]),
            pltpu.make_async_copy(
                recv_ref.at[local, :, pl.ds(2 * width, 2 * slab + 128)], side, load_sem.at[2]),
        ]
        for copy in copies:
            copy.start()
        for copy in copies:
            copy.wait()

    def forward(local):
        cut_x, cut_dy, weight_block = side[:, :slab], side[:, slab : 2 * slab], side[:, 2 * slab :]

        def joiner(j):
            source = q // EXTRA * CELL + j * EXTRA + q % EXTRA
            return jnp.where(r == source, 1.0, 0.0).astype(BF16)

        for j in range(SLABS):
            columns = pl.ds(j * slab, slab)
            x_all[rows:, columns] = mm(joiner(j), cut_x).astype(BF16)
            dy_all[rows:, columns] = mm(joiner(j), cut_dy).astype(BF16)
        weight_whole = weight_block[:, 0:1].astype(F32)
        weight_cut = mm(joiner(0), weight_block)[:, 64:65]
        weight = jnp.concatenate([weight_whole, weight_cut], axis=0)
        step = total // 3
        probs = []
        for i in range(3):
            here = pl.ds(i * step, step)
            dy = dy_all[here, :]
            pre = mm(x_all[here, :], w_gu[...])
            gate_pre, up_pre = pre[:, :units], pre[:, units:]
            raw = mm(dy, w_down[...], 1, 1)
            sig = jax.nn.sigmoid(gate_pre)
            activated = gate_pre * sig
            slope = sig * (1.0 + gate_pre * (1.0 - sig))
            hidden = (activated * up_pre).astype(BF16)
            probs.append(jnp.sum(hidden.astype(F32) * raw, axis=1, keepdims=True))
            w = weight[i * step : (i + 1) * step, :]
            pushed = w * raw
            hidden_all[here, :] = hidden
            gu_grad[here, :units] = (pushed * up_pre * slope).astype(BF16)
            gu_grad[here, units:] = (pushed * activated).astype(BF16)
            dy_all[here, :] = (w * dy.astype(F32)).astype(BF16)
        prob = jnp.concatenate(probs, axis=0)
        same = (r_t // CELL == q_t // EXTRA) & (r_t % EXTRA == q_t % EXTRA)
        prob_cut = jnp.broadcast_to(prob[rows:, :], (extra, 128)).astype(BF16)
        prob_cut = mm(jnp.where(same, 1.0, 0.0).astype(BF16), prob_cut)
        lane = iota((rows, 128), 1)
        back_send[local, :, width + slab :] = jnp.where(lane < 64, prob[:rows, :], prob_cut).astype(BF16)

    def weight_grads(local):
        part = width // groups
        pieces = 2 * units // part

        def one(k, carry):
            g = lax.rem(z + half + k, groups)
            columns = pl.ds(pl.multiple_of(g * part, part), part)
            gu = (grad_scale * mm(x_all[:, columns], gu_grad[...], 0, 0)).astype(BF16)
            for s in range(pieces):
                grads[local, g, s * part : (s + 1) * part, :] = gu[:, s * part : (s + 1) * part]
            down = grad_scale * mm(hidden_all[...], dy_all[:, columns], 0, 0)
            grads[local, g, pieces * part :, :] = down.astype(BF16)
            return carry

        one(0, 0)
        ring_step(local, 0)
        lax.fori_loop(1, groups, one, 0)

    def input_grads(local):
        piece = rows // 2
        for i in range(2):
            here = pl.ds(i * piece, piece)
            back_send[local, here, :width] = mm(gu_grad[here, :], w_gu[...], 1, 1).astype(BF16)
        dx = mm(gu_grad[rows:, :], w_gu[...], 1, 1).astype(BF16)
        cut_back = 0.0
        for j in range(SLABS):
            source = q_t // EXTRA * CELL + j * EXTRA + q_t % EXTRA
            splitter = jnp.where(r_t == source, 1.0, 0.0).astype(BF16)
            cut_back = cut_back + mm(splitter, dx[:, j * slab : (j + 1) * slab])
        back_send[local, :, width : width + slab] = cut_back.astype(BF16)

    load_weights(0, True)
    barrier = pltpu.get_barrier_semaphore()

    def greet(i, carry):
        pl.semaphore_signal(barrier, inc=1, device_id=(z, lax.rem(me + i, owners)), device_id_type=MESH)
        return carry

    lax.fori_loop(1, owners, greet, 0)
    pl.semaphore_signal(barrier, inc=1, device_id=ring_right, device_id_type=MESH)
    pl.semaphore_signal(barrier, inc=1, device_id=ring_left, device_id_type=MESH)
    pack(0, local_count, owners, routes_ref, weights_ref, count_ref, x_ref, dy_ref, send.at[0])
    pl.semaphore_wait(barrier, owners + 1)
    spread_out(send, recv_ref, own_sem, send_sem, recv_sem, 0)
    pack(1, local_count, owners, routes_ref, weights_ref, count_ref, x_ref, dy_ref, send.at[1])
    all_of(send, recv_ref, send_sem, recv_sem, 0).wait_send()
    spread_out(send, recv_ref, own_sem, send_sem, recv_sem, 1)

    load_weights(0, False)
    load_rows(0)
    forward(0)
    weight_grads(0)
    input_grads(0)
    spread_out(back_send, back_recv, back_own_sem, back_send_sem, back_recv_sem, 0)
    load_weights(1, True)
    for step in range(1, half):
        ring_step(0, step)

    load_weights(1, False)
    load_rows(1)
    forward(1)
    weight_grads(1)
    input_grads(1)
    spread_out(back_send, back_recv, back_own_sem, back_send_sem, back_recv_sem, 1)
    ring_end(0)
    for step in range(1, half):
        ring_step(1, step)
    for local in range(local_count):
        all_of(back_send, back_recv, back_send_sem, back_recv_sem, local).wait_recv()
        wait_own(back_send, back_recv, back_own_sem, local)
    combine(local_count, owners, routes_ref, [back_recv.at[i] for i in range(local_count)], dx_ref, prob_ref)
    ring_end(1)
    all_of(send, recv_ref, send_sem, recv_sem, 1).wait_send()
    for local in range(local_count):
        all_of(back_send, back_recv, back_send_sem, back_recv_sem, local).wait_send()
        for step in range(half):
            hop(local, step, True).wait_send()
            hop(local, step, False).wait_send()


def combine(local_count, owners, routes_ref, back_refs, dx_ref, prob_ref):
    top_k, tokens = routes_ref.shape
    width = dx_ref.shape[1]
    slab = width // SLABS
    routes_t = routes_ref[...]
    dx = 0.0
    cut_dx = [0.0] * SLABS
    probs = [0.0] * top_k
    for local in range(local_count):
        back_ref = back_refs[local]
        wanted, spread, place, whole, cut = cell_tables(routes_t, local, local_count, owners)
        dx = dx + mm(jnp.where(whole, 1.0, 0.0).astype(BF16), back_ref[:, :width], 0, 0)
        for j in range(SLABS):
            here = jnp.where(cut & (place // EXTRA == j), 1.0, 0.0).astype(BF16)
            cut_dx[j] = cut_dx[j] + mm(here, back_ref[:, width : width + slab], 0, 0)
        block = back_ref[:, width + slab :].astype(F32)
        held = jnp.where(whole, block[:, 0:1], 0.0)
        held = held + jnp.where(cut & (place // EXTRA == 0), block[:, 64:65], 0.0)
        by_owner = mm(spread, held.astype(BF16), 0, 0)
        for k in range(top_k):
            mine = jnp.where(routes_t[k : k + 1, :] == wanted, by_owner, 0.0)
            probs[k] = probs[k] + jnp.sum(mine, axis=0, keepdims=True)
    for j in range(SLABS):
        columns = slice(j * slab, (j + 1) * slab)
        dx_ref[:, columns] = (dx[:, columns] + cut_dx[j]).astype(BF16)
    for k in range(top_k):
        prob_ref[k : k + 1, :] = probs[k]


def vmem():
    return pl.BlockSpec(memory_space=pltpu.VMEM)


def shards(
    inputs, out_grad, route_weights, routes, response_counts, gate_weight, up_weight, down_weight
):
    tokens, width = inputs.shape
    top_k = routes.shape[1]
    local_count, _, units = gate_weight.shape
    owners = lax.axis_size("expert")
    groups = lax.axis_size("dp")
    grad_scale = (tokens * top_k * groups / local_count) ** (-0.5)
    rows = owners * CELL
    extra = owners * EXTRA
    slab = width // SLABS
    half = groups // 2
    send_width = 2 * width + 2 * slab + 128
    back_width = width + slab + 128
    part = width // groups
    block = 3 * units
    dma = pltpu.SemaphoreType.DMA
    in_grad, prob_t, gate_grad, up_grad, down_grad, _ = pl.pallas_call(
        functools.partial(whole_kernel, grad_scale),
        out_shape=(
            jax.ShapeDtypeStruct((tokens, width), BF16),
            jax.ShapeDtypeStruct((top_k, tokens), F32),
            jax.ShapeDtypeStruct((local_count, part, units), BF16),
            jax.ShapeDtypeStruct((local_count, part, units), BF16),
            jax.ShapeDtypeStruct((local_count, units, part), BF16),
            jax.ShapeDtypeStruct((local_count, rows, send_width), BF16),
        ),
        in_specs=[vmem(), vmem(), pl.BlockSpec(memory_space=pltpu.SMEM), vmem(), vmem()]
        + [pl.BlockSpec(memory_space=pl.ANY)] * 3,
        out_specs=(vmem(), vmem(), vmem(), vmem(), vmem(), pl.BlockSpec(memory_space=pl.ANY)),
        scratch_shapes=[
            pltpu.VMEM((local_count, rows, send_width), BF16),
            pltpu.VMEM((rows + extra, width), BF16),
            pltpu.VMEM((rows + extra, width), BF16),
            pltpu.VMEM((rows, 2 * slab + 128), BF16),
            pltpu.VMEM((rows + extra, 2 * units), BF16),
            pltpu.VMEM((rows + extra, units), BF16),
            pltpu.VMEM((width, 2 * units), BF16),
            pltpu.VMEM((units, width), BF16),
            pltpu.VMEM((local_count, groups, block, part), BF16),
            pltpu.VMEM((local_count, half, block, part), BF16),
            pltpu.VMEM((local_count, half, block, part), BF16),
            pltpu.VMEM((local_count, rows, back_width), BF16),
            pltpu.VMEM((local_count, rows, back_width), BF16),
            dma((3,)), dma((2,)), dma((2,)), dma((2,)), dma((2,)), dma((2,)), dma((2,)),
            dma((3,)), dma((2, 2, half)), dma((2, 2, half)),
        ],
        compiler_params=pltpu.CompilerParams(
            vmem_limit_bytes=VMEM_LIMIT, collective_id=0, has_side_effects=True
        ),
        name="whole",
    )(routes.T, route_weights.T, response_counts, inputs, out_grad, gate_weight, up_weight, down_weight)
    route_weight_grad = prob_t.T.astype(BF16)
    return in_grad, gate_grad, up_grad, down_grad, route_weight_grad


def solution(mesh):
    tokens = P(("dp", "expert"), None)
    return jax.shard_map(
        shards,
        mesh=mesh,
        in_specs=(
            tokens, tokens, tokens, tokens,
            P(("dp", "expert")),
            P("expert", None, None), P("expert", None, None), P("expert", None, None),
        ),
        out_specs=(
            tokens, P("expert", "dp", None), P("expert", "dp", None), P("expert", None, "dp"), tokens,
        ),
        check_vma=False,
    )
```

```python
import functools

import jax
import jax.numpy as jnp
from jax import lax
from jax.experimental import pallas as pl
from jax.experimental.pallas import tpu as pltpu
from jax.sharding import PartitionSpec as P

F32 = jnp.float32
BF16 = jnp.bfloat16
I32 = jnp.int32
CELL = 16
EXTRA = 2
SLABS = CELL // EXTRA
VMEM_LIMIT = 61 * 1024 * 1024
MESH = pl.DeviceIdType.MESH


def iota(shape, dim):
    return lax.broadcasted_iota(I32, shape, dim)


def mm(a, b, ca=1, cb=0):
    return lax.dot_general(a, b, (((ca,), (cb,)), ((), ())), preferred_element_type=F32)


def cell_tables(routes_t, wanted):
    top_k, tokens = routes_t.shape
    owners = wanted.shape[0]
    names = jnp.zeros((owners, tokens), F32)
    for k in range(top_k):
        names = names + jnp.where(routes_t[k : k + 1, :] == wanted, 1.0, 0.0)
    before = jnp.where(iota((tokens, tokens), 0) < iota((tokens, tokens), 1), 1.0, 0.0)
    rank = mm(names.astype(BF16), before.astype(BF16))
    rank = jnp.where(names > 0.5, rank, -1.0)
    rows = owners * CELL
    spread = jnp.where(iota((rows, owners), 0) // CELL == iota((rows, owners), 1), 1.0, 0.0)
    spread = spread.astype(BF16)
    rank_rows = mm(spread, rank.astype(BF16)).astype(I32)
    place = iota((rows, tokens), 0) % CELL
    whole = rank_rows == place
    cut = rank_rows == CELL + place % EXTRA
    return spread, place, whole, cut


def pack(wanted, meta, rows_in, out_ref, top):
    tokens = meta.shape[1]
    width = rows_in.shape[1]
    slab = width // 2 // SLABS
    routes_t = meta[:top, :].astype(F32).astype(I32)
    weights_t = meta[top:, :].astype(F32)
    spread, place, whole, cut = cell_tables(routes_t, wanted)
    combine_weights = jnp.zeros(wanted.shape, F32)
    for k in range(top):
        combine_weights = combine_weights + jnp.where(
            routes_t[k : k + 1, :] == wanted, weights_t[k : k + 1, :], 0.0
        )
    weight_rows = mm(spread, combine_weights.astype(BF16))
    out_ref[:, :width] = mm(jnp.where(whole, 1.0, 0.0).astype(BF16), rows_in).astype(BF16)
    picks = [jnp.where(cut & (place // EXTRA == j), 1.0, 0.0).astype(BF16) for j in range(SLABS)]
    slabs = [
        jnp.concatenate(
            [rows_in[:, h * (width // 2) + j * slab : h * (width // 2) + (j + 1) * slab] for h in range(2)],
            axis=1,
        )
        for j in range(SLABS)
    ]
    parts = mm(jnp.concatenate(picks, axis=1), jnp.concatenate(slabs, axis=0))
    out_ref[:, width : width + 2 * slab] = parts.astype(BF16)
    whole_weight = jnp.sum(jnp.where(whole, weight_rows, 0.0), axis=1, keepdims=True)
    cut_weight = jnp.sum(jnp.where(cut, weight_rows, 0.0), axis=1, keepdims=True)
    lane = iota((out_ref.shape[0], 128), 1)
    out_ref[:, width + 2 * slab :] = jnp.where(lane < 64, whole_weight, cut_weight).astype(BF16)


def whole_kernel(
    grad_scale, across,
    routes_ref, meta_ref, count_ref, x_ref, dy_ref, wg_ref, wu_ref, wd_ref,
    dx_ref, prob_ref, gate_ref, up_ref, down_ref, recv_ref,
    stage, meta, send, x_all, dy_all, side, gu_grad, hidden_all, w_gu, w_down, grads, flow_r, flow_l,
    back_recv,
    stage_send_sem, stage_recv_sem, meta_send_sem, meta_recv_sem,
    load_sem, own_sem, send_sem, recv_sem, back_own_sem, back_send_sem, back_recv_sem,
    weight_sem, flow_send_sem, flow_recv_sem,
):
    owners, groups = lax.axis_size("expert"), lax.axis_size("dp")
    me, z = lax.axis_index("expert"), lax.axis_index("dp")
    back_send = send.at[0]
    local_count, width, units = wg_ref.shape
    top_k, tokens = routes_ref.shape
    rows = owners * CELL
    extra = owners * EXTRA
    total = rows + extra
    slab = width // SLABS
    half = groups // 2
    block = grads.shape[2]
    top = block // 2
    ring_right = (lax.rem(z + 1, groups), me)
    ring_left = (lax.rem(z + groups - 1, groups), me)
    beside = (z, lax.rem(me + 1, owners))
    half_width = width // 2
    half_slab = slab // 2
    up_down = owners // 2 // across
    y, x, core = me // (2 * across), (me // 2) % across, me % 2
    sources = (across, up_down)
    mine = (x, y)
    targets = (2 * up_down, 2 * across)
    my_target = (2 * y + core, 2 * x + core)
    sent_width = (2 * half_width + 2 * half_slab + 128, 2 * half_width + 2 * half_slab)
    offset = (0, sent_width[0])

    def source_index(way, s):
        return (y * across + s) * 2 + core if way == 0 else (s * across + x) * 2 + core

    def target_index(way, d):
        return ((d // 2) * across + x) * 2 + d % 2 if way == 0 else (y * across + d // 2) * 2 + d % 2

    def fill_stage():
        live = iota((tokens, 1), 0) >= tokens - count_ref[0]
        for way in range(2):
            columns = pl.ds(way * half_width, half_width)
            stage[way, mine[way], :, :half_width] = x_ref[:, columns]
            dy = jnp.where(live, dy_ref[:, columns].astype(F32), 0.0).astype(BF16)
            stage[way, mine[way], :, half_width:] = dy
            meta[way, mine[way]] = meta_ref[...]

    def first_hop():
        for way in range(2):

            def tell(i, carry, way=way):
                s = lax.rem(mine[way] + i, sources[way])
                pltpu.make_async_remote_copy(
                    src_ref=meta.at[way, mine[way]], dst_ref=meta.at[way, mine[way]],
                    send_sem=meta_send_sem.at[way], recv_sem=meta_recv_sem.at[way],
                    device_id=(z, source_index(way, s)), device_id_type=MESH,
                ).start()
                return carry

            lax.fori_loop(1, sources[way], tell, 0)
        pieces = 8
        size = 2 * half_width // pieces
        for c in range(pieces):
            for way in range(2):

                def one(i, carry, way=way, columns=pl.ds(c * size, size)):
                    s = lax.rem(mine[way] + i, sources[way])
                    pltpu.make_async_remote_copy(
                        src_ref=stage.at[way, mine[way], :, columns],
                        dst_ref=stage.at[way, mine[way], :, columns],
                        send_sem=stage_send_sem.at[way], recv_sem=stage_recv_sem.at[way],
                        device_id=(z, source_index(way, s)), device_id_type=MESH,
                    ).start()
                    return carry

                lax.fori_loop(1, sources[way], one, 0)

    def first_hop_copies(way):
        others = pl.ds(0, sources[way] - 1)
        return [
            pltpu.make_async_remote_copy(
                src_ref=array.at[way, others], dst_ref=array.at[way, others],
                send_sem=sends.at[way], recv_sem=recvs.at[way],
                device_id=beside, device_id_type=MESH,
            )
            for array, sends, recvs in (
                (meta, meta_send_sem, meta_recv_sem), (stage, stage_send_sem, stage_recv_sem),
            )
            if sources[way] > 1
        ]

    def pack_way(local, way):
        count = targets[way]
        wanted = target_index(way, iota((count, tokens), 0)) * local_count + local

        def one(s, carry):
            here = pl.ds(pl.multiple_of(s * count * CELL, CELL), count * CELL)
            pack(wanted, meta[way, s], stage[way, s], send.at[local, way, here], meta.shape[2] // 2)
            return carry

        lax.fori_loop(0, sources[way], one, 0)

    def cell_copy(local, way, s, d, columns):
        return (
            send.at[local, way, pl.ds((s * targets[way] + d) * CELL, CELL), columns],
            recv_ref.at[
                local, pl.ds(source_index(way, s) * CELL, CELL),
                pl.ds(offset[way] + columns.start, columns.size),
            ],
        )

    def second_hop(local):
        for way in range(2):

            def keep(s, carry, way=way):
                a, b = cell_copy(local, way, s, my_target[way], pl.ds(0, sent_width[way]))
                pltpu.make_async_copy(a, b, own_sem.at[local, way]).start()
                return carry

            lax.fori_loop(0, sources[way], keep, 0)
        pieces = 4
        for c in range(pieces):

            def one(k, carry, ways=(0, 1), c=c):
                for way in ways:
                    tiles = sent_width[way] // 128
                    low, high = tiles * c // pieces * 128, tiles * (c + 1) // pieces * 128
                    others = targets[way] - 1
                    d = lax.rem(my_target[way] + 1 + lax.rem(k, others), targets[way])
                    a, b = cell_copy(local, way, k // others, d, pl.ds(low, high - low))
                    pltpu.make_async_remote_copy(
                        src_ref=a, dst_ref=b,
                        send_sem=send_sem.at[local, way], recv_sem=recv_sem.at[local, way],
                        device_id=(z, target_index(way, d)), device_id_type=MESH,
                    ).start()
                return carry

            counts = [sources[way] * (targets[way] - 1) for way in range(2)]
            if counts[0] == counts[1]:
                lax.fori_loop(0, counts[0], one, 0)
            else:
                for way in range(2):
                    lax.fori_loop(0, counts[way], functools.partial(one, ways=(way,)), 0)

    def second_hop_copy(local, way):
        most = pl.ds(0, sources[way] * (targets[way] - 1) * CELL)
        return pltpu.make_async_remote_copy(
            src_ref=send.at[local, way, most, pl.ds(0, sent_width[way])],
            dst_ref=recv_ref.at[local, most, pl.ds(offset[way], sent_width[way])],
            send_sem=send_sem.at[local, way], recv_sem=recv_sem.at[local, way],
            device_id=beside, device_id_type=MESH,
        )

    def second_hop_sent(local):
        for way in range(2):
            second_hop_copy(local, way).wait_send()

    def second_hop_arrived(local):
        for way in range(2):
            second_hop_copy(local, way).wait_recv()
            most = pl.ds(0, sources[way] * CELL)
            pltpu.make_async_copy(
                send.at[local, way, most, pl.ds(0, sent_width[way])],
                recv_ref.at[local, most, pl.ds(offset[way], sent_width[way])],
                own_sem.at[local, way],
            ).wait()

    def load_weights(local, start):
        copies = [
            pltpu.make_async_copy(wg_ref.at[local], w_gu.at[:, pl.ds(0, units)], weight_sem.at[0]),
            pltpu.make_async_copy(wu_ref.at[local], w_gu.at[:, pl.ds(units, units)], weight_sem.at[1]),
            pltpu.make_async_copy(wd_ref.at[local], w_down, weight_sem.at[2]),
        ]
        for copy in copies:
            if start:
                copy.start()
            else:
                copy.wait()

    def spread_out(source, target, own, sends, recvs, local):
        pltpu.make_async_copy(
            source.at[local, pl.ds(me * CELL, CELL)], target.at[local, pl.ds(me * CELL, CELL)],
            own.at[local],
        ).start()

        tiles = source.shape[2] // 128
        pieces = max(1, tiles // 4)
        for c in range(pieces):
            low, high = tiles * c // pieces * 128, tiles * (c + 1) // pieces * 128

            def one(i, carry, columns=pl.ds(low, high - low)):
                to = lax.rem(me + i, owners)
                pltpu.make_async_remote_copy(
                    src_ref=source.at[local, pl.ds(to * CELL, CELL), columns],
                    dst_ref=target.at[local, pl.ds(me * CELL, CELL), columns],
                    send_sem=sends.at[local],
                    recv_sem=recvs.at[local],
                    device_id=(z, to),
                    device_id_type=MESH,
                ).start()
                return carry

            lax.fori_loop(1, owners, one, 0)

    def all_of(source, target, sends, recvs, local):
        most = pl.ds(0, rows - CELL)
        return pltpu.make_async_remote_copy(
            src_ref=source.at[local, most], dst_ref=target.at[local, most],
            send_sem=sends.at[local], recv_sem=recvs.at[local],
            device_id=beside, device_id_type=MESH,
        )

    def wait_own(source, target, own, local):
        pltpu.make_async_copy(
            source.at[local, pl.ds(me * CELL, CELL)], target.at[local, pl.ds(me * CELL, CELL)],
            own.at[local],
        ).wait()

    def hops_of(right, part):
        return half if right == (part == 0) else half - 1

    chains = [c for c in ((True, 0), (False, 1), (True, 1), (False, 0)) if hops_of(*c) > 0]

    def chain_target(right, part, step):
        away = hops_of(right, part) - step
        return lax.rem(z + (away if right else groups - away), groups)

    def hop(local, right, part, step):
        flow = flow_r if right else flow_l
        here = pl.ds(part * top, top)
        if step == 0:
            source = grads.at[local, chain_target(right, part, 0), here]
        else:
            source = flow.at[local, step - 1, here]
        way = 0 if right else 1
        return pltpu.make_async_remote_copy(
            src_ref=source, dst_ref=flow.at[local, step, here],
            send_sem=flow_send_sem.at[local, way, part, step],
            recv_sem=flow_recv_sem.at[local, way, part, step],
            device_id=ring_right if right else ring_left, device_id_type=MESH,
        )

    def add_rows(out, terms):
        count = terms[0].shape[0]
        piece = count // 4

        def one(i, carry):
            here = pl.ds(pl.multiple_of(i * piece, piece), piece)
            value = terms[0][here, :].astype(F32)
            for term in terms[1:]:
                value = value + term[here, :].astype(F32)
            out[here, :] = value.astype(BF16)
            return carry

        lax.fori_loop(0, 4, one, 0)

    def ring_step(local, step):
        for right, part in chains:
            if step < hops_of(right, part):
                hop(local, right, part, step - 1).wait_recv()
                held = (flow_r if right else flow_l).at[local, step - 1, pl.ds(part * top, top)]
                own = grads.at[local, chain_target(right, part, step), pl.ds(part * top, top)]
                add_rows(held, [held, own])
                hop(local, right, part, step).start()

    def ring_end(local):
        for right, half_at in chains:
            hop(local, right, half_at, hops_of(right, half_at) - 1).wait_recv()
        part = width // groups
        pieces = 2 * units // part

        def summed(low, count):
            here = pl.ds(low, count)
            value = grads[local, z, here, :].astype(F32)
            for right, half_at in chains:
                if half_at == low // top:
                    flow = flow_r if right else flow_l
                    value = value + flow[local, hops_of(right, half_at) - 1, here, :].astype(F32)
            return value.astype(BF16)

        step = part // 4
        for i in range(4 * pieces):
            value = summed(i * step, step)
            at, here = i // 4 * part, slice(i % 4 * step, (i % 4 + 1) * step)
            in_gate = max(0, min(part, units - at))
            if in_gate > 0:
                gate_ref[local, here, at : at + in_gate] = value[:, :in_gate]
            if in_gate < part:
                up_ref[local, here, at + in_gate - units : at + part - units] = value[:, in_gate:]
        for i in range(units // step):
            down_ref[local, i * step : (i + 1) * step, :] = summed(pieces * part + i * step, step)

    side_width = 2 * half_slab + 128
    r = iota((extra, rows), 1)
    q = iota((extra, rows), 0)
    r_t = iota((rows, extra), 0)
    q_t = iota((rows, extra), 1)

    def load_rows(local):
        second_hop_arrived(local)
        copies = []
        for way in range(2):
            here = pl.ds(way * half_width, half_width)
            for at, (target, low, size) in enumerate((
                (x_all.at[pl.ds(0, rows), here], 0, half_width),
                (dy_all.at[pl.ds(0, rows), here], half_width, half_width),
                (side.at[:, pl.ds(way * side_width, sent_width[way] - 2 * half_width)],
                 2 * half_width, sent_width[way] - 2 * half_width),
            )):
                copies.append(pltpu.make_async_copy(
                    recv_ref.at[local, :, pl.ds(offset[way] + low, size)], target, load_sem.at[way, at]))
        for copy in copies:
            copy.start()
        for copy in copies:
            copy.wait()

    def forward(local):
        side_rows = side[...]
        weight_whole = side_rows[:, 2 * half_slab : 2 * half_slab + 1].astype(F32)

        def joiner(j):
            source = q // EXTRA * CELL + j * EXTRA + q % EXTRA
            return jnp.where(r == source, 1.0, 0.0).astype(BF16)

        for j in range(SLABS):
            joined = mm(joiner(j), side_rows)
            if j == 0:
                weight_cut = joined[:, 2 * half_slab + 64 : 2 * half_slab + 65]
            for way in range(2):
                columns = pl.ds(way * half_width + j * half_slab, half_slab)
                low = way * side_width
                x_all[rows:, columns] = joined[:, low : low + half_slab].astype(BF16)
                dy_all[rows:, columns] = joined[:, low + half_slab : low + 2 * half_slab].astype(BF16)
        weight = jnp.concatenate([weight_whole, weight_cut], axis=0)
        step = total // 3
        probs = []
        for i in range(3):
            here = pl.ds(i * step, step)
            dy = dy_all[here, :]
            pre = mm(x_all[here, :], w_gu[...])
            gate_pre, up_pre = pre[:, :units], pre[:, units:]
            raw = mm(dy, w_down[...], 1, 1)
            sig = jax.nn.sigmoid(gate_pre)
            activated = gate_pre * sig
            slope = sig * (1.0 + gate_pre * (1.0 - sig))
            hidden = (activated * up_pre).astype(BF16)
            probs.append(jnp.sum(hidden.astype(F32) * raw, axis=1, keepdims=True))
            w = weight[i * step : (i + 1) * step, :]
            pushed = w * raw
            hidden_all[here, :] = hidden
            gu_grad[here, :units] = (pushed * up_pre * slope).astype(BF16)
            gu_grad[here, units:] = (pushed * activated).astype(BF16)
            dy_all[here, :] = (w * dy.astype(F32)).astype(BF16)
        prob = jnp.concatenate(probs, axis=0)
        same = (r_t // CELL == q_t // EXTRA) & (r_t % EXTRA == q_t % EXTRA)
        prob_cut = jnp.broadcast_to(prob[rows:, :], (extra, 128)).astype(BF16)
        prob_cut = mm(jnp.where(same, 1.0, 0.0).astype(BF16), prob_cut)
        lane = iota((rows, 128), 1)
        back_send[local, :, width + slab :] = jnp.where(lane < 64, prob[:rows, :], prob_cut).astype(BF16)

    def weight_grads(local):
        part = width // groups
        pieces = 2 * units // part

        def one(k, carry):
            turn = lax.rem(k, 2)
            g = lax.rem(z + half + groups + (1 - 2 * turn) * ((k + turn) // 2), groups)
            columns = pl.ds(pl.multiple_of(g * part, part), part)
            gu = (grad_scale * mm(x_all[:, columns], gu_grad[...], 0, 0)).astype(BF16)
            for s in range(pieces):
                grads[local, g, s * part : (s + 1) * part, :] = gu[:, s * part : (s + 1) * part]
            down = grad_scale * mm(hidden_all[...], dy_all[:, columns], 0, 0)
            grads[local, g, pieces * part :, :] = down.astype(BF16)
            return carry

        one(0, 0)
        for chain in chains[:2]:
            hop(local, *chain, 0).start()
        if half > 1:
            one(1, 0)
            one(2, 0)
            for chain in chains[2:]:
                hop(local, *chain, 0).start()
        lax.fori_loop(min(half * 2 - 1, 3), groups, one, 0)

    def input_grads(local):
        piece = rows // 2
        for i in range(2):
            here = pl.ds(i * piece, piece)
            back_send[local, here, :width] = mm(gu_grad[here, :], w_gu[...], 1, 1).astype(BF16)
        dx = mm(gu_grad[rows:, :], w_gu[...], 1, 1).astype(BF16)
        cut_back = 0.0
        for j in range(SLABS):
            source = q_t // EXTRA * CELL + j * EXTRA + q_t % EXTRA
            splitter = jnp.where(r_t == source, 1.0, 0.0).astype(BF16)
            cut_back = cut_back + mm(splitter, dx[:, j * slab : (j + 1) * slab])
        back_send[local, :, width : width + slab] = cut_back.astype(BF16)

    load_weights(0, True)
    barrier = pltpu.get_barrier_semaphore()

    def greet(i, carry):
        pl.semaphore_signal(barrier, inc=1, device_id=(z, lax.rem(me + i, owners)), device_id_type=MESH)
        return carry

    lax.fori_loop(1, owners, greet, 0)
    pl.semaphore_signal(barrier, inc=1, device_id=ring_right, device_id_type=MESH)
    pl.semaphore_signal(barrier, inc=1, device_id=ring_left, device_id_type=MESH)
    fill_stage()
    pl.semaphore_wait(barrier, owners + 1)
    first_hop()
    for way in range(2):
        for copy in first_hop_copies(way):
            copy.wait_recv()
        pack_way(0, way)
    second_hop(0)
    for way in range(2):
        pack_way(1, way)
    second_hop_sent(0)
    second_hop(1)

    load_weights(0, False)
    load_rows(0)
    forward(0)
    weight_grads(0)
    input_grads(0)
    spread_out(back_send, back_recv, back_own_sem, back_send_sem, back_recv_sem, 0)
    load_weights(1, True)
    for step in range(1, half):
        ring_step(0, step)

    load_weights(1, False)
    load_rows(1)
    forward(1)
    weight_grads(1)
    input_grads(1)
    spread_out(back_send, back_recv, back_own_sem, back_send_sem, back_recv_sem, 1)
    ring_end(0)
    for step in range(1, half):
        ring_step(1, step)
    for local in range(local_count):
        all_of(back_send, back_recv, back_send_sem, back_recv_sem, local).wait_recv()
        wait_own(back_send, back_recv, back_own_sem, local)
    combine(local_count, owners, routes_ref, [back_recv.at[i] for i in range(local_count)], dx_ref, prob_ref)
    ring_end(1)
    second_hop_sent(1)
    for way in range(2):
        for copy in first_hop_copies(way):
            copy.wait_send()
    for local in range(local_count):
        all_of(back_send, back_recv, back_send_sem, back_recv_sem, local).wait_send()
        for chain in chains:
            for step in range(hops_of(*chain)):
                hop(local, *chain, step).wait_send()


def combine(local_count, owners, routes_ref, back_refs, dx_ref, prob_ref):
    top_k, tokens = routes_ref.shape
    width = dx_ref.shape[1]
    slab = width // SLABS
    routes_t = routes_ref[...]
    dx = 0.0
    cut_dx = [0.0] * SLABS
    probs = [0.0] * top_k
    for local in range(local_count):
        back_ref = back_refs[local]
        wanted = iota((owners, tokens), 0) * local_count + local
        spread, place, whole, cut = cell_tables(routes_t, wanted)
        dx = dx + mm(jnp.where(whole, 1.0, 0.0).astype(BF16), back_ref[:, :width], 0, 0)
        for j in range(SLABS):
            here = jnp.where(cut & (place // EXTRA == j), 1.0, 0.0).astype(BF16)
            cut_dx[j] = cut_dx[j] + mm(here, back_ref[:, width : width + slab], 0, 0)
        block = back_ref[:, width + slab :].astype(F32)
        held = jnp.where(whole, block[:, 0:1], 0.0)
        held = held + jnp.where(cut & (place // EXTRA == 0), block[:, 64:65], 0.0)
        by_owner = mm(spread, held.astype(BF16), 0, 0)
        for k in range(top_k):
            mine = jnp.where(routes_t[k : k + 1, :] == wanted, by_owner, 0.0)
            probs[k] = probs[k] + jnp.sum(mine, axis=0, keepdims=True)
    for j in range(SLABS):
        columns = slice(j * slab, (j + 1) * slab)
        dx_ref[:, columns] = (dx[:, columns] + cut_dx[j]).astype(BF16)
    for k in range(top_k):
        prob_ref[k : k + 1, :] = probs[k]


def finish_kernel(prob_ref, *refs):
    count = len(refs) // 2
    for source, target in zip(refs[:count], refs[count : 2 * count]):
        target[...] = source[...]
    refs[-1][...] = prob_ref[...].T.astype(BF16)


def vmem():
    return pl.BlockSpec(memory_space=pltpu.VMEM)


def shards(
    inputs, out_grad, route_weights, routes, response_counts, gate_weight, up_weight, down_weight
):
    tokens, width = inputs.shape
    top_k = routes.shape[1]
    local_count, _, units = gate_weight.shape
    owners = lax.axis_size("expert")
    groups = lax.axis_size("dp")
    grad_scale = (tokens * top_k * groups / local_count) ** (-0.5)
    rows = owners * CELL
    extra = owners * EXTRA
    slab = width // SLABS
    half = groups // 2
    send_width = width + slab + 128
    across = 1 << ((owners // 2).bit_length() // 2)
    longest = max(across, owners // 2 // across)
    back_width = width + slab + 128
    part = width // groups
    block = 3 * units
    dma = pltpu.SemaphoreType.DMA
    routes_t = routes.T
    meta = jnp.concatenate([routes_t.astype(BF16), route_weights.T], axis=0)
    in_grad, prob_t, gate_grad, up_grad, down_grad, _ = pl.pallas_call(
        functools.partial(whole_kernel, grad_scale, across),
        out_shape=(
            jax.ShapeDtypeStruct((tokens, width), BF16),
            jax.ShapeDtypeStruct((top_k, tokens), F32),
            jax.ShapeDtypeStruct((local_count, part, units), BF16),
            jax.ShapeDtypeStruct((local_count, part, units), BF16),
            jax.ShapeDtypeStruct((local_count, units, part), BF16),
            jax.ShapeDtypeStruct((local_count, rows, 2 * send_width - 128), BF16),
        ),
        in_specs=[vmem(), vmem(), pl.BlockSpec(memory_space=pltpu.SMEM), vmem(), vmem()]
        + [pl.BlockSpec(memory_space=pl.ANY)] * 3,
        out_specs=(vmem(), vmem(), vmem(), vmem(), vmem(), pl.BlockSpec(memory_space=pl.ANY)),
        scratch_shapes=[
            pltpu.VMEM((2, longest, tokens, width), BF16),
            pltpu.VMEM((2, longest, 2 * top_k, tokens), BF16),
            pltpu.VMEM((local_count, 2, rows, send_width), BF16),
            pltpu.VMEM((rows + extra, width), BF16),
            pltpu.VMEM((rows + extra, width), BF16),
            pltpu.VMEM((rows, 2 * slab + 128), BF16),
            pltpu.VMEM((rows + extra, 2 * units), BF16),
            pltpu.VMEM((rows + extra, units), BF16),
            pltpu.VMEM((width, 2 * units), BF16),
            pltpu.VMEM((units, width), BF16),
            pltpu.VMEM((local_count, groups, block, part), BF16),
            pltpu.VMEM((local_count, half, block, part), BF16),
            pltpu.VMEM((local_count, half, block, part), BF16),
            pltpu.VMEM((local_count, rows, back_width), BF16),
            dma((2,)), dma((2,)), dma((2,)), dma((2,)),
            dma((2, 3)), dma((2, 2)), dma((2, 2)), dma((2, 2)), dma((2,)), dma((2,)), dma((2,)),
            dma((3,)), dma((2, 2, 2, half)), dma((2, 2, 2, half)),
        ],
        compiler_params=pltpu.CompilerParams(
            vmem_limit_bytes=VMEM_LIMIT, collective_id=0, has_side_effects=True
        ),
        name="whole",
    )(routes_t, meta, response_counts, inputs, out_grad, gate_weight, up_weight, down_weight)
    results = (in_grad, gate_grad, up_grad, down_grad)
    return pl.pallas_call(
        finish_kernel,
        out_shape=tuple(jax.ShapeDtypeStruct(a.shape, BF16) for a in results)
        + (jax.ShapeDtypeStruct((tokens, top_k), BF16),),
        in_specs=[vmem()] * 5,
        out_specs=tuple([vmem()] * 5),
        name="finish",
    )(prob_t, *results)


def solution(mesh):
    tokens = P(("dp", "expert"), None)
    return jax.shard_map(
        shards,
        mesh=mesh,
        in_specs=(
            tokens, tokens, tokens, tokens,
            P(("dp", "expert")),
            P("expert", None, None), P("expert", None, None), P("expert", None, None),
        ),
        out_specs=(
            tokens, P("expert", "dp", None), P("expert", "dp", None), P("expert", None, "dp"), tokens,
        ),
        check_vma=False,
    )
```

```python
import functools

import jax
import jax.numpy as jnp
from jax import lax
from jax.experimental import pallas as pl
from jax.experimental.pallas import tpu as pltpu
from jax.sharding import PartitionSpec as P

F32 = jnp.float32
BF16 = jnp.bfloat16
I32 = jnp.int32
CELL = 16
EXTRA = 2
SLABS = CELL // EXTRA
VMEM_LIMIT = 61 * 1024 * 1024
MESH = pl.DeviceIdType.MESH


def iota(shape, dim):
    return lax.broadcasted_iota(I32, shape, dim)


def mm(a, b, ca=1, cb=0):
    return lax.dot_general(a, b, (((ca,), (cb,)), ((), ())), preferred_element_type=F32)


def cell_tables(routes_t, wanted):
    top_k, tokens = routes_t.shape
    owners = wanted.shape[0]
    names = jnp.zeros((owners, tokens), F32)
    for k in range(top_k):
        names = names + jnp.where(routes_t[k : k + 1, :] == wanted, 1.0, 0.0)
    before = jnp.where(iota((tokens, tokens), 0) < iota((tokens, tokens), 1), 1.0, 0.0)
    rank = mm(names.astype(BF16), before.astype(BF16))
    rank = jnp.where(names > 0.5, rank, -1.0)
    rows = owners * CELL
    spread = jnp.where(iota((rows, owners), 0) // CELL == iota((rows, owners), 1), 1.0, 0.0)
    spread = spread.astype(BF16)
    rank_rows = mm(spread, rank.astype(BF16)).astype(I32)
    place = iota((rows, tokens), 0) % CELL
    whole = rank_rows == place
    cut = rank_rows == CELL + place % EXTRA
    return spread, place, whole, cut


def pack(wanted, meta, rows_in, out_ref, top, part):
    tokens = meta.shape[1]
    width = rows_in.shape[1]
    slab = width // 2 // SLABS
    routes_t = meta[:top, :].astype(F32).astype(I32)
    weights_t = meta[top:, :].astype(F32)
    spread, place, whole, cut = cell_tables(routes_t, wanted)
    combine_weights = jnp.zeros(wanted.shape, F32)
    for k in range(top):
        combine_weights = combine_weights + jnp.where(
            routes_t[k : k + 1, :] == wanted, weights_t[k : k + 1, :], 0.0
        )
    weight_rows = mm(spread, combine_weights.astype(BF16))
    here = pl.ds(part * (width // 2), width // 2)
    out_ref[:, here] = mm(jnp.where(whole, 1.0, 0.0).astype(BF16), rows_in[:, here]).astype(BF16)
    if part == 0:
        return
    picks = [jnp.where(cut & (place // EXTRA == j), 1.0, 0.0).astype(BF16) for j in range(SLABS)]
    slabs = [
        jnp.concatenate(
            [rows_in[:, h * (width // 2) + j * slab : h * (width // 2) + (j + 1) * slab] for h in range(2)],
            axis=1,
        )
        for j in range(SLABS)
    ]
    parts = mm(jnp.concatenate(picks, axis=1), jnp.concatenate(slabs, axis=0))
    out_ref[:, width : width + 2 * slab] = parts.astype(BF16)
    whole_weight = jnp.sum(jnp.where(whole, weight_rows, 0.0), axis=1, keepdims=True)
    cut_weight = jnp.sum(jnp.where(cut, weight_rows, 0.0), axis=1, keepdims=True)
    lane = iota((out_ref.shape[0], 128), 1)
    out_ref[:, width + 2 * slab :] = jnp.where(lane < 64, whole_weight, cut_weight).astype(BF16)


def whole_kernel(
    grad_scale, across,
    routes_ref, meta_ref, count_ref, x_ref, dy_ref, wg_ref, wu_ref, wd_ref,
    dx_ref, prob_ref, gate_ref, up_ref, down_ref, recv_ref,
    stage, meta, send, x_all, dy_all, side, gu_grad, hidden_all, w_gu, w_down, grads, flow_r, flow_l,
    back_recv,
    stage_send_sem, stage_recv_sem, meta_send_sem, meta_recv_sem,
    load_sem, own_sem, send_sem, recv_sem, back_own_sem, back_send_sem, back_recv_sem,
    weight_sem, flow_send_sem, flow_recv_sem,
):
    owners, groups = lax.axis_size("expert"), lax.axis_size("dp")
    me, z = lax.axis_index("expert"), lax.axis_index("dp")
    back_send = send.at[0]
    local_count, width, units = wg_ref.shape
    top_k, tokens = routes_ref.shape
    rows = owners * CELL
    extra = owners * EXTRA
    total = rows + extra
    slab = width // SLABS
    half = groups // 2
    block = grads.shape[2]
    top = block // 2
    ring_right = (lax.rem(z + 1, groups), me)
    ring_left = (lax.rem(z + groups - 1, groups), me)
    beside = (z, lax.rem(me + 1, owners))
    half_width = width // 2
    half_slab = slab // 2
    up_down = owners // 2 // across
    y, x, core = me // (2 * across), (me // 2) % across, me % 2
    sources = (across, up_down)
    mine = (x, y)
    targets = (2 * up_down, 2 * across)
    my_target = (2 * y + core, 2 * x + core)
    sent_width = (2 * half_width + 2 * half_slab + 128, 2 * half_width + 2 * half_slab)
    offset = (0, sent_width[0])

    def source_index(way, s):
        return (y * across + s) * 2 + core if way == 0 else (s * across + x) * 2 + core

    def target_index(way, d):
        return ((d // 2) * across + x) * 2 + d % 2 if way == 0 else (y * across + d // 2) * 2 + d % 2

    def fill_stage():
        live = iota((tokens, 1), 0) >= tokens - count_ref[0]
        for way in range(2):
            columns = pl.ds(way * half_width, half_width)
            stage[way, mine[way], :, :half_width] = x_ref[:, columns]
            dy = jnp.where(live, dy_ref[:, columns].astype(F32), 0.0).astype(BF16)
            stage[way, mine[way], :, half_width:] = dy
            meta[way, mine[way]] = meta_ref[...]

    def first_hop():
        for way in range(2):

            def tell(i, carry, way=way):
                s = lax.rem(mine[way] + i, sources[way])
                pltpu.make_async_remote_copy(
                    src_ref=meta.at[way, mine[way]], dst_ref=meta.at[way, mine[way]],
                    send_sem=meta_send_sem.at[way], recv_sem=meta_recv_sem.at[way],
                    device_id=(z, source_index(way, s)), device_id_type=MESH,
                ).start()
                return carry

            lax.fori_loop(1, sources[way], tell, 0)
        pieces = 8
        size = 2 * half_width // pieces
        for c in range(pieces):
            for way in range(2):

                def one(i, carry, way=way, columns=pl.ds(c * size, size), part=c * 2 // pieces):
                    s = lax.rem(mine[way] + i, sources[way])
                    pltpu.make_async_remote_copy(
                        src_ref=stage.at[way, mine[way], :, columns],
                        dst_ref=stage.at[way, mine[way], :, columns],
                        send_sem=stage_send_sem.at[way, part], recv_sem=stage_recv_sem.at[way, part],
                        device_id=(z, source_index(way, s)), device_id_type=MESH,
                    ).start()
                    return carry

                lax.fori_loop(1, sources[way], one, 0)

    def first_hop_copies(way, part):
        if sources[way] == 1:
            return []
        others = pl.ds(0, sources[way] - 1)
        rows_part = stage.at[way, others, :, pl.ds(part * half_width, half_width)]
        copies = [
            pltpu.make_async_remote_copy(
                src_ref=rows_part, dst_ref=rows_part,
                send_sem=stage_send_sem.at[way, part], recv_sem=stage_recv_sem.at[way, part],
                device_id=beside, device_id_type=MESH,
            )
        ]
        if part == 0:
            copies.append(
                pltpu.make_async_remote_copy(
                    src_ref=meta.at[way, others], dst_ref=meta.at[way, others],
                    send_sem=meta_send_sem.at[way], recv_sem=meta_recv_sem.at[way],
                    device_id=beside, device_id_type=MESH,
                )
            )
        return copies

    def pack_way(local, way, part):
        count = targets[way]
        wanted = target_index(way, iota((count, tokens), 0)) * local_count + local

        def one(s, carry):
            here = pl.ds(pl.multiple_of(s * count * CELL, CELL), count * CELL)
            pack(wanted, meta[way, s], stage.at[way, s], send.at[local, way, here], meta.shape[2] // 2, part)
            return carry

        lax.fori_loop(0, sources[way], one, 0)

    def cell_copy(local, way, s, d, columns):
        return (
            send.at[local, way, pl.ds((s * targets[way] + d) * CELL, CELL), columns],
            recv_ref.at[
                local, pl.ds(source_index(way, s) * CELL, CELL),
                pl.ds(offset[way] + columns.start, columns.size),
            ],
        )

    def second_hop(local, part):
        for way in range(2 * part):

            def keep(s, carry, way=way):
                a, b = cell_copy(local, way, s, my_target[way], pl.ds(0, sent_width[way]))
                pltpu.make_async_copy(a, b, own_sem.at[local, way]).start()
                return carry

            lax.fori_loop(0, sources[way], keep, 0)
        pieces = 2 + part
        for c in range(pieces):

            def one(k, carry, ways=(0, 1), c=c):
                for way in ways:
                    first = half_width // 128 * part
                    tiles = (sent_width[way] // 128 if part else half_width // 128) - first
                    low = (first + tiles * c // pieces) * 128
                    high = (first + tiles * (c + 1) // pieces) * 128
                    others = targets[way] - 1
                    d = lax.rem(my_target[way] + 1 + lax.rem(k, others), targets[way])
                    a, b = cell_copy(local, way, k // others, d, pl.ds(low, high - low))
                    pltpu.make_async_remote_copy(
                        src_ref=a, dst_ref=b,
                        send_sem=send_sem.at[local, way], recv_sem=recv_sem.at[local, way],
                        device_id=(z, target_index(way, d)), device_id_type=MESH,
                    ).start()
                return carry

            counts = [sources[way] * (targets[way] - 1) for way in range(2)]
            if counts[0] == counts[1]:
                lax.fori_loop(0, counts[0], one, 0)
            else:
                for way in range(2):
                    lax.fori_loop(0, counts[way], functools.partial(one, ways=(way,)), 0)

    def second_hop_copy(local, way):
        most = pl.ds(0, sources[way] * (targets[way] - 1) * CELL)
        return pltpu.make_async_remote_copy(
            src_ref=send.at[local, way, most, pl.ds(0, sent_width[way])],
            dst_ref=recv_ref.at[local, most, pl.ds(offset[way], sent_width[way])],
            send_sem=send_sem.at[local, way], recv_sem=recv_sem.at[local, way],
            device_id=beside, device_id_type=MESH,
        )

    def second_hop_sent(local):
        for way in range(2):
            second_hop_copy(local, way).wait_send()

    def second_hop_arrived(local):
        for way in range(2):
            second_hop_copy(local, way).wait_recv()
            most = pl.ds(0, sources[way] * CELL)
            pltpu.make_async_copy(
                send.at[local, way, most, pl.ds(0, sent_width[way])],
                recv_ref.at[local, most, pl.ds(offset[way], sent_width[way])],
                own_sem.at[local, way],
            ).wait()

    def load_weights(local, start):
        copies = [
            pltpu.make_async_copy(wg_ref.at[local], w_gu.at[:, pl.ds(0, units)], weight_sem.at[0]),
            pltpu.make_async_copy(wu_ref.at[local], w_gu.at[:, pl.ds(units, units)], weight_sem.at[1]),
            pltpu.make_async_copy(wd_ref.at[local], w_down, weight_sem.at[2]),
        ]
        for copy in copies:
            if start:
                copy.start()
            else:
                copy.wait()

    def spread_out(source, target, own, sends, recvs, local):
        pltpu.make_async_copy(
            source.at[local, pl.ds(me * CELL, CELL)], target.at[local, pl.ds(me * CELL, CELL)],
            own.at[local],
        ).start()

        tiles = source.shape[2] // 128
        pieces = max(1, tiles // 4)
        for c in range(pieces):
            low, high = tiles * c // pieces * 128, tiles * (c + 1) // pieces * 128

            def one(i, carry, columns=pl.ds(low, high - low)):
                to = lax.rem(me + i, owners)
                pltpu.make_async_remote_copy(
                    src_ref=source.at[local, pl.ds(to * CELL, CELL), columns],
                    dst_ref=target.at[local, pl.ds(me * CELL, CELL), columns],
                    send_sem=sends.at[local],
                    recv_sem=recvs.at[local],
                    device_id=(z, to),
                    device_id_type=MESH,
                ).start()
                return carry

            lax.fori_loop(1, owners, one, 0)

    def all_of(source, target, sends, recvs, local):
        most = pl.ds(0, rows - CELL)
        return pltpu.make_async_remote_copy(
            src_ref=source.at[local, most], dst_ref=target.at[local, most],
            send_sem=sends.at[local], recv_sem=recvs.at[local],
            device_id=beside, device_id_type=MESH,
        )

    def wait_own(source, target, own, local):
        pltpu.make_async_copy(
            source.at[local, pl.ds(me * CELL, CELL)], target.at[local, pl.ds(me * CELL, CELL)],
            own.at[local],
        ).wait()

    def hops_of(right, part):
        return half if right == (part == 0) else half - 1

    chains = [c for c in ((True, 0), (False, 1), (True, 1), (False, 0)) if hops_of(*c) > 0]

    def chain_target(right, part, step):
        away = hops_of(right, part) - step
        return lax.rem(z + (away if right else groups - away), groups)

    def hop(local, right, part, step):
        flow = flow_r if right else flow_l
        here = pl.ds(part * top, top)
        if step == 0:
            source = grads.at[local, chain_target(right, part, 0), here]
        else:
            source = flow.at[local, step - 1, here]
        way = 0 if right else 1
        return pltpu.make_async_remote_copy(
            src_ref=source, dst_ref=flow.at[local, step, here],
            send_sem=flow_send_sem.at[local, way, part, step],
            recv_sem=flow_recv_sem.at[local, way, part, step],
            device_id=ring_right if right else ring_left, device_id_type=MESH,
        )

    def add_rows(out, terms):
        count = terms[0].shape[0]
        piece = count // 4

        def one(i, carry):
            here = pl.ds(pl.multiple_of(i * piece, piece), piece)
            value = terms[0][here, :].astype(F32)
            for term in terms[1:]:
                value = value + term[here, :].astype(F32)
            out[here, :] = value.astype(BF16)
            return carry

        lax.fori_loop(0, 4, one, 0)

    def ring_step(local, step):
        for right, part in chains:
            if step < hops_of(right, part):
                hop(local, right, part, step - 1).wait_recv()
                held = (flow_r if right else flow_l).at[local, step - 1, pl.ds(part * top, top)]
                own = grads.at[local, chain_target(right, part, step), pl.ds(part * top, top)]
                add_rows(held, [held, own])
                hop(local, right, part, step).start()

    def ring_end(local):
        for right, half_at in chains:
            hop(local, right, half_at, hops_of(right, half_at) - 1).wait_recv()
        part = width // groups
        pieces = 2 * units // part

        def summed(low, count):
            here = pl.ds(low, count)
            value = grads[local, z, here, :].astype(F32)
            for right, half_at in chains:
                if half_at == low // top:
                    flow = flow_r if right else flow_l
                    value = value + flow[local, hops_of(right, half_at) - 1, here, :].astype(F32)
            return value.astype(BF16)

        step = part // 4
        for i in range(4 * pieces):
            value = summed(i * step, step)
            at, here = i // 4 * part, slice(i % 4 * step, (i % 4 + 1) * step)
            in_gate = max(0, min(part, units - at))
            if in_gate > 0:
                gate_ref[local, here, at : at + in_gate] = value[:, :in_gate]
            if in_gate < part:
                up_ref[local, here, at + in_gate - units : at + part - units] = value[:, in_gate:]
        for i in range(units // step):
            down_ref[local, i * step : (i + 1) * step, :] = summed(pieces * part + i * step, step)

    side_width = 2 * half_slab + 128
    r = iota((extra, rows), 1)
    q = iota((extra, rows), 0)
    r_t = iota((rows, extra), 0)
    q_t = iota((rows, extra), 1)

    def load_rows(local):
        second_hop_arrived(local)
        copies = []
        for way in range(2):
            here = pl.ds(way * half_width, half_width)
            for at, (target, low, size) in enumerate((
                (x_all.at[pl.ds(0, rows), here], 0, half_width),
                (dy_all.at[pl.ds(0, rows), here], half_width, half_width),
                (side.at[:, pl.ds(way * side_width, sent_width[way] - 2 * half_width)],
                 2 * half_width, sent_width[way] - 2 * half_width),
            )):
                copies.append(pltpu.make_async_copy(
                    recv_ref.at[local, :, pl.ds(offset[way] + low, size)], target, load_sem.at[way, at]))
        for copy in copies:
            copy.start()
        for copy in copies:
            copy.wait()

    def forward(local):
        side_rows = side[...]
        weight_whole = side_rows[:, 2 * half_slab : 2 * half_slab + 1].astype(F32)

        def joiner(j):
            source = q // EXTRA * CELL + j * EXTRA + q % EXTRA
            return jnp.where(r == source, 1.0, 0.0).astype(BF16)

        for j in range(SLABS):
            joined = mm(joiner(j), side_rows)
            if j == 0:
                weight_cut = joined[:, 2 * half_slab + 64 : 2 * half_slab + 65]
            for way in range(2):
                columns = pl.ds(way * half_width + j * half_slab, half_slab)
                low = way * side_width
                x_all[rows:, columns] = joined[:, low : low + half_slab].astype(BF16)
                dy_all[rows:, columns] = joined[:, low + half_slab : low + 2 * half_slab].astype(BF16)
        weight = jnp.concatenate([weight_whole, weight_cut], axis=0)
        step = total // 3
        probs = []
        for i in range(3):
            here = pl.ds(i * step, step)
            dy = dy_all[here, :]
            pre = mm(x_all[here, :], w_gu[...])
            gate_pre, up_pre = pre[:, :units], pre[:, units:]
            raw = mm(dy, w_down[...], 1, 1)
            sig = jax.nn.sigmoid(gate_pre)
            activated = gate_pre * sig
            slope = sig * (1.0 + gate_pre * (1.0 - sig))
            hidden = (activated * up_pre).astype(BF16)
            probs.append(jnp.sum(hidden.astype(F32) * raw, axis=1, keepdims=True))
            w = weight[i * step : (i + 1) * step, :]
            pushed = w * raw
            hidden_all[here, :] = hidden
            gu_grad[here, :units] = (pushed * up_pre * slope).astype(BF16)
            gu_grad[here, units:] = (pushed * activated).astype(BF16)
            dy_all[here, :] = (w * dy.astype(F32)).astype(BF16)
        prob = jnp.concatenate(probs, axis=0)
        same = (r_t // CELL == q_t // EXTRA) & (r_t % EXTRA == q_t % EXTRA)
        prob_cut = jnp.broadcast_to(prob[rows:, :], (extra, 128)).astype(BF16)
        prob_cut = mm(jnp.where(same, 1.0, 0.0).astype(BF16), prob_cut)
        lane = iota((rows, 128), 1)
        back_send[local, :, width + slab :] = jnp.where(lane < 64, prob[:rows, :], prob_cut).astype(BF16)

    def weight_grads(local):
        part = width // groups
        pieces = 2 * units // part

        def one(k, carry):
            turn = lax.rem(k, 2)
            g = lax.rem(z + half + groups + (1 - 2 * turn) * ((k + turn) // 2), groups)
            columns = pl.ds(pl.multiple_of(g * part, part), part)
            gu = (grad_scale * mm(x_all[:, columns], gu_grad[...], 0, 0)).astype(BF16)
            for s in range(pieces):
                grads[local, g, s * part : (s + 1) * part, :] = gu[:, s * part : (s + 1) * part]
            down = grad_scale * mm(hidden_all[...], dy_all[:, columns], 0, 0)
            grads[local, g, pieces * part :, :] = down.astype(BF16)
            return carry

        one(0, 0)
        for chain in chains[:2]:
            hop(local, *chain, 0).start()
        if half > 1:
            one(1, 0)
            one(2, 0)
            for chain in chains[2:]:
                hop(local, *chain, 0).start()
        lax.fori_loop(min(half * 2 - 1, 3), groups, one, 0)

    def input_grads(local):
        piece = rows // 2
        for i in range(2):
            here = pl.ds(i * piece, piece)
            back_send[local, here, :width] = mm(gu_grad[here, :], w_gu[...], 1, 1).astype(BF16)
        dx = mm(gu_grad[rows:, :], w_gu[...], 1, 1).astype(BF16)
        cut_back = 0.0
        for j in range(SLABS):
            source = q_t // EXTRA * CELL + j * EXTRA + q_t % EXTRA
            splitter = jnp.where(r_t == source, 1.0, 0.0).astype(BF16)
            cut_back = cut_back + mm(splitter, dx[:, j * slab : (j + 1) * slab])
        back_send[local, :, width : width + slab] = cut_back.astype(BF16)

    load_weights(0, True)
    barrier = pltpu.get_barrier_semaphore()

    def greet(i, carry):
        pl.semaphore_signal(barrier, inc=1, device_id=(z, lax.rem(me + i, owners)), device_id_type=MESH)
        return carry

    lax.fori_loop(1, owners, greet, 0)
    pl.semaphore_signal(barrier, inc=1, device_id=ring_right, device_id_type=MESH)
    pl.semaphore_signal(barrier, inc=1, device_id=ring_left, device_id_type=MESH)
    fill_stage()
    pl.semaphore_wait(barrier, owners + 1)
    first_hop()
    for part in range(2):
        for way in range(2):
            for copy in first_hop_copies(way, part):
                copy.wait_recv()
            pack_way(0, way, part)
        second_hop(0, part)
    for part in range(2):
        for way in range(2):
            pack_way(1, way, part)
    second_hop_sent(0)
    second_hop(1, 0)
    second_hop(1, 1)

    load_weights(0, False)
    load_rows(0)
    forward(0)
    weight_grads(0)
    input_grads(0)
    load_weights(1, True)
    for step in range(1, half - 1):
        ring_step(0, step)
    load_weights(1, False)
    load_rows(1)
    spread_out(back_send, back_recv, back_own_sem, back_send_sem, back_recv_sem, 0)
    forward(1)
    ring_step(0, half - 1)
    weight_grads(1)
    input_grads(1)
    spread_out(back_send, back_recv, back_own_sem, back_send_sem, back_recv_sem, 1)
    ring_end(0)
    for step in range(1, half):
        ring_step(1, step)
    for local in range(local_count):
        all_of(back_send, back_recv, back_send_sem, back_recv_sem, local).wait_recv()
        wait_own(back_send, back_recv, back_own_sem, local)
    combine(local_count, owners, routes_ref, [back_recv.at[i] for i in range(local_count)], dx_ref, prob_ref)
    ring_end(1)
    second_hop_sent(1)
    for way in range(2):
        for copy in first_hop_copies(way, 0) + first_hop_copies(way, 1):
            copy.wait_send()
    for local in range(local_count):
        all_of(back_send, back_recv, back_send_sem, back_recv_sem, local).wait_send()
        for chain in chains:
            for step in range(hops_of(*chain)):
                hop(local, *chain, step).wait_send()


def combine(local_count, owners, routes_ref, back_refs, dx_ref, prob_ref):
    top_k, tokens = routes_ref.shape
    width = dx_ref.shape[1]
    slab = width // SLABS
    routes_t = routes_ref[...]
    dx = 0.0
    cut_dx = [0.0] * SLABS
    probs = [0.0] * top_k
    for local in range(local_count):
        back_ref = back_refs[local]
        wanted = iota((owners, tokens), 0) * local_count + local
        spread, place, whole, cut = cell_tables(routes_t, wanted)
        dx = dx + mm(jnp.where(whole, 1.0, 0.0).astype(BF16), back_ref[:, :width], 0, 0)
        for j in range(SLABS):
            here = jnp.where(cut & (place // EXTRA == j), 1.0, 0.0).astype(BF16)
            cut_dx[j] = cut_dx[j] + mm(here, back_ref[:, width : width + slab], 0, 0)
        block = back_ref[:, width + slab :].astype(F32)
        held = jnp.where(whole, block[:, 0:1], 0.0)
        held = held + jnp.where(cut & (place // EXTRA == 0), block[:, 64:65], 0.0)
        by_owner = mm(spread, held.astype(BF16), 0, 0)
        for k in range(top_k):
            mine = jnp.where(routes_t[k : k + 1, :] == wanted, by_owner, 0.0)
            probs[k] = probs[k] + jnp.sum(mine, axis=0, keepdims=True)
    for j in range(SLABS):
        columns = slice(j * slab, (j + 1) * slab)
        dx_ref[:, columns] = (dx[:, columns] + cut_dx[j]).astype(BF16)
    for k in range(top_k):
        prob_ref[k : k + 1, :] = probs[k]


def finish_kernel(prob_ref, *refs):
    count = len(refs) // 2
    for source, target in zip(refs[:count], refs[count : 2 * count]):
        target[...] = source[...]
    refs[-1][...] = prob_ref[...].T.astype(BF16)


def vmem():
    return pl.BlockSpec(memory_space=pltpu.VMEM)


def shards(
    inputs, out_grad, route_weights, routes, response_counts, gate_weight, up_weight, down_weight
):
    tokens, width = inputs.shape
    top_k = routes.shape[1]
    local_count, _, units = gate_weight.shape
    owners = lax.axis_size("expert")
    groups = lax.axis_size("dp")
    grad_scale = (tokens * top_k * groups / local_count) ** (-0.5)
    rows = owners * CELL
    extra = owners * EXTRA
    slab = width // SLABS
    half = groups // 2
    send_width = width + slab + 128
    across = 1 << ((owners // 2).bit_length() // 2)
    longest = max(across, owners // 2 // across)
    back_width = width + slab + 128
    part = width // groups
    block = 3 * units
    dma = pltpu.SemaphoreType.DMA
    routes_t = routes.T
    meta = jnp.concatenate([routes_t.astype(BF16), route_weights.T], axis=0)
    in_grad, prob_t, gate_grad, up_grad, down_grad, _ = pl.pallas_call(
        functools.partial(whole_kernel, grad_scale, across),
        out_shape=(
            jax.ShapeDtypeStruct((tokens, width), BF16),
            jax.ShapeDtypeStruct((top_k, tokens), F32),
            jax.ShapeDtypeStruct((local_count, part, units), BF16),
            jax.ShapeDtypeStruct((local_count, part, units), BF16),
            jax.ShapeDtypeStruct((local_count, units, part), BF16),
            jax.ShapeDtypeStruct((local_count, rows, 2 * send_width - 128), BF16),
        ),
        in_specs=[vmem(), vmem(), pl.BlockSpec(memory_space=pltpu.SMEM), vmem(), vmem()]
        + [pl.BlockSpec(memory_space=pl.ANY)] * 3,
        out_specs=(vmem(), vmem(), vmem(), vmem(), vmem(), pl.BlockSpec(memory_space=pl.ANY)),
        scratch_shapes=[
            pltpu.VMEM((2, longest, tokens, width), BF16),
            pltpu.VMEM((2, longest, 2 * top_k, tokens), BF16),
            pltpu.VMEM((local_count, 2, rows, send_width), BF16),
            pltpu.VMEM((rows + extra, width), BF16),
            pltpu.VMEM((rows + extra, width), BF16),
            pltpu.VMEM((rows, 2 * slab + 128), BF16),
            pltpu.VMEM((rows + extra, 2 * units), BF16),
            pltpu.VMEM((rows + extra, units), BF16),
            pltpu.VMEM((width, 2 * units), BF16),
            pltpu.VMEM((units, width), BF16),
            pltpu.VMEM((local_count, groups, block, part), BF16),
            pltpu.VMEM((local_count, half, block, part), BF16),
            pltpu.VMEM((local_count, half, block, part), BF16),
            pltpu.VMEM((local_count, rows, back_width), BF16),
            dma((2, 2)), dma((2, 2)), dma((2,)), dma((2,)),
            dma((2, 3)), dma((2, 2)), dma((2, 2)), dma((2, 2)), dma((2,)), dma((2,)), dma((2,)),
            dma((3,)), dma((2, 2, 2, half)), dma((2, 2, 2, half)),
        ],
        compiler_params=pltpu.CompilerParams(
            vmem_limit_bytes=VMEM_LIMIT, collective_id=0, has_side_effects=True
        ),
        name="whole",
    )(routes_t, meta, response_counts, inputs, out_grad, gate_weight, up_weight, down_weight)
    results = (in_grad, gate_grad, up_grad, down_grad)
    return pl.pallas_call(
        finish_kernel,
        out_shape=tuple(jax.ShapeDtypeStruct(a.shape, BF16) for a in results)
        + (jax.ShapeDtypeStruct((tokens, top_k), BF16),),
        in_specs=[vmem()] * 5,
        out_specs=tuple([vmem()] * 5),
        name="finish",
    )(prob_t, *results)


def solution(mesh):
    tokens = P(("dp", "expert"), None)
    return jax.shard_map(
        shards,
        mesh=mesh,
        in_specs=(
            tokens, tokens, tokens, tokens,
            P(("dp", "expert")),
            P("expert", None, None), P("expert", None, None), P("expert", None, None),
        ),
        out_specs=(
            tokens, P("expert", "dp", None), P("expert", "dp", None), P("expert", None, "dp"), tokens,
        ),
        check_vma=False,
    )
```
